256 devices in a mesh: dp: 4 (over y), ctx: 16 (over z, core), tp: 4 (over x).
Axes of the slice: x: 4, y: 4, z: 8, core: 2. Of those that a mesh axis runs over, the one named last changes fastest.
Arguments:
- head_input: bfloat16 [4, 4096, 4096], P('dp', 'ctx', 'tp'), may hold values from -6 to 6
- write_vectors: bfloat16 [4, 4096, 512], P('dp', 'ctx', 'tp'), may hold values from -0.5 to 0.5
- read_vectors: bfloat16 [4, 4096, 512], P('dp', 'ctx', 'tp'), may hold values from -0.5 to 0.5
- log_decay: float32 [4, 64, 4096], P('dp', 'tp', 'ctx'), may hold values from -0.8 to 0, as said below
- cotangent: bfloat16 [4, 4096, 4096], P('dp', 'ctx', 'tp'), may hold values from -8 to 8
- out_weight: bfloat16 [4096, 4096], P(('dp', 'ctx'), 'tp'), may hold values from -0.09375 to 0.09375
- scale_exponent: int32 [128, 4096], P(('dp', 'ctx'), 'tp'), may hold values from -1 to 1
Outputs:
- grad_input: bfloat16 [4, 4096, 4096], P('dp', 'ctx', 'tp')
- grad_write: bfloat16 [4, 4096, 512], P('dp', 'ctx', 'tp')
- grad_read: bfloat16 [4, 4096, 512], P('dp', 'ctx', 'tp')
- grad_weight: float32 [4096, 4096], P(('dp', 'ctx'), 'tp')
The draws below stay inside these ranges and needn't reach their ends.
Inputs may be any that keep to these rules, and one draw needn't show every extreme that they name: `log_decay`: every entry is negative.
All inputs are finite; a program needn't handle non-finite values.
Results may differ from the reference program's by a relative error of at most 0.015.
Values may be sent and summed in bfloat16 or wider, within the bound.
No kernel may reach another device: no remote copies, remote signals or barrier semaphores. Data moves between devices by JAX's collectives and lax.ppermute only.
A program may use at most 128 MiB of HBM per device.

```python
import jax
import jax.numpy as jnp
from jax import lax

D = 4096
HEADS = 64
GROUPS = 4
HEAD_DIM = 64
STATE = 128
BLOCK = 256
SCALE_BLOCK = 32
NSEQ = 4
SEQUENCE_LENGTH = 4096


def draw_log_decay(key, part):
    key = jax.random.fold_in(key, 7)
    random_subkeys = jax.random.split(key, 6)
    dimensions = (NSEQ, HEADS, SEQUENCE_LENGTH)
    slow_heads = jax.random.bernoulli(random_subkeys[0], 0.5, (HEADS,))
    multiplier = jnp.exp(jax.random.uniform(random_subkeys[3], dimensions, jnp.float32, jnp.log(0.5), jnp.log(2.0)))
    fast_rate = jnp.exp(jax.random.uniform(random_subkeys[1], (HEADS,), jnp.float32, jnp.log(1.0 / 50.0), jnp.log(1.0 / 30.0)))
    slow_rate = jnp.exp(jax.random.uniform(random_subkeys[2], (HEADS,), jnp.float32, jnp.log(0.05), jnp.log(0.5))) / SEQUENCE_LENGTH
    each_position = jnp.where(slow_heads, slow_rate, fast_rate)
    transfer_groups = jax.random.bernoulli(random_subkeys[4], 3.0 / SEQUENCE_LENGTH, dimensions)
    transfer_depth = jax.random.uniform(random_subkeys[5], dimensions, jnp.float32, 0.22, 0.7)
    return -(each_position[None, :, None] * multiplier + jnp.where(transfer_groups, transfer_depth, 0.0))


def place_ends(values, key, low, high):
    place = [jax.random.randint(jax.random.fold_in(key, axis), (), 0, length) for axis, length in enumerate(values.shape)]
    longest = values.shape.index(max(values.shape))
    neighbour = place[:longest] + [(place[longest] + 1) % values.shape[longest]] + place[longest + 1:]
    return values.at[tuple(place)].set(low).at[tuple(neighbour)].set(high)


def raised(drawn, rng, source, target, parts, factor):
    def block_of(position):
        return (jnp.arange(drawn.shape[position]) // (drawn.shape[position] // parts)).reshape((-1,) + (1,) * (drawn.ndim - 1 - position))

    one_side = jax.random.permutation(rng, parts)[block_of(target)]
    other_side = (block_of(target) + parts // 2) % parts
    return jnp.where((block_of(source) == one_side) | (block_of(source) == other_side), factor * drawn, drawn)


def steps_of(stream_key, dims, shards, least, top_value):
    level = 1.0
    for position, blocks in shards:
        draws = jax.random.uniform(jax.random.fold_in(jax.random.fold_in(stream_key, 6), position), (blocks,), jnp.float32, least / len(shards), top_value / len(shards))
        level = level * jnp.repeat(jnp.exp(draws), dims[position] // blocks).reshape((-1,) + (1,) * (len(dims) - 1 - position))
    return level


def normal_values(stream_key, shape, spread, limit, cuts=(), held_as=jnp.bfloat16):
    loudness = steps_of(stream_key, shape, cuts, -0.22, 0.18) if cuts else 1.0
    result = jax.random.normal(stream_key, shape, jnp.float32) * spread * loudness
    return jnp.minimum(jnp.maximum(result, -limit), limit).astype(held_as)


def bell_draw_with(rng, extent, width, bound, cuts, heavy, kind=jnp.bfloat16):
    drawn = width * jax.random.normal(rng, extent, jnp.float32)
    if cuts:
        drawn = drawn * steps_of(rng, extent, cuts, -0.22, 0.18)
    return jnp.clip(raised(drawn, jax.random.fold_in(rng, 3), *heavy), -bound, bound).astype(kind)


def setup_inputs(seed: int = 0) -> dict:
    keys = jax.random.split(jax.random.key(seed), 8)
    return {
        "head_input": normal_values(keys[0], (NSEQ, SEQUENCE_LENGTH, HEADS * HEAD_DIM), 1.0, 6.0, ((0, 4), (1, 16), (2, 4))),
        "write_vectors": normal_values(keys[1], (NSEQ, SEQUENCE_LENGTH, GROUPS * STATE), STATE ** -0.5, 0.5, ((0, 4), (1, 16), (2, 4))),
        "read_vectors": normal_values(keys[2], (NSEQ, SEQUENCE_LENGTH, GROUPS * STATE), STATE ** -0.5, 0.5, ((0, 4), (1, 16), (2, 4))),
        "log_decay": draw_log_decay(jax.random.fold_in(keys[7], 71), 0),
        "cotangent": bell_draw_with(keys[4], (NSEQ, SEQUENCE_LENGTH, D), 1.0, 8.0, ((0, 4), (1, 16), (2, 4)), (1, 2, 16, 2.0)),
        "out_weight": normal_values(keys[5], (D, HEADS * HEAD_DIM), D ** -0.5, 0.09375, ((0, 64), (1, 4))),
        "scale_exponent": place_ends(jax.random.randint(keys[6], (D // SCALE_BLOCK, HEADS * HEAD_DIM), -1, 2), jax.random.fold_in(keys[6], 1), -1, 1).astype(jnp.int32),
    }


def group_pass(inputs, writes, readers, log_rates, grad_rows):
    length = inputs.shape[0]
    blocks = length // BLOCK
    per_group = inputs.shape[1]
    maximum_precision = lax.Precision.HIGHEST
    values = inputs.astype(jnp.float32).reshape(blocks, BLOCK, per_group, HEAD_DIM)
    write_f = writes.astype(jnp.float32).reshape(blocks, BLOCK, STATE)
    read_function = readers.astype(jnp.float32).reshape(blocks, BLOCK, STATE)
    gradient_function = grad_rows.astype(jnp.float32).reshape(blocks, BLOCK, per_group, HEAD_DIM)
    cumulative = jnp.cumsum(log_rates.reshape(per_group, blocks, BLOCK), axis=-1)
    block_ends = cumulative[..., -1:]
    to_end = jnp.exp(block_ends - cumulative)
    since_beginning = jnp.exp(cumulative)
    decays = jnp.exp(cumulative[..., -1])
    offsets = jnp.arange(BLOCK)
    causal = offsets[:, None] >= offsets[None, :]
    within = jnp.exp(jnp.where(causal, cumulative[..., :, None] - cumulative[..., None, :], -jnp.inf))
    intersections = jnp.einsum("ktn,kun->ktu", read_function, write_f, precision=maximum_precision)
    mixing = within * intersections[None]
    written = jnp.einsum("hku,kuhp,kun->khpn", to_end, values, write_f, precision=maximum_precision)
    produced_rows = jnp.einsum("dra,radj,rat->rdjt", since_beginning, gradient_function, read_function, precision=maximum_precision)

    def step_forward(carry, pieces):
        decay_now, fresh = pieces
        return decay_now[:, None, None] * carry + fresh, carry

    def step_backward(carry, pieces):
        decay_now, fresh = pieces
        return fresh + decay_now[:, None, None] * carry, carry

    start_state = jnp.zeros((per_group, HEAD_DIM, STATE), jnp.float32)
    _, entering = lax.scan(step_forward, start_state, (jnp.transpose(decays), written))
    _, leaving = lax.scan(step_backward, start_state, (jnp.transpose(decays), produced_rows), reverse=True)
    mixer = jnp.einsum("hktu,kuhp->kthp", mixing, values, precision=maximum_precision)
    mixer = mixer + jnp.einsum("hkt,khpn,ktn->kthp", since_beginning, entering, read_function, precision=maximum_precision)
    pair_dots = jnp.einsum("kvhp,kuhp->hkvu", gradient_function, values, precision=maximum_precision)
    weighted = within * pair_dots
    grad_in = jnp.einsum("hkvt,kvhp->kthp", mixing, gradient_function, precision=maximum_precision)
    grad_in = grad_in + jnp.einsum("hkt,khpn,ktn->kthp", to_end, leaving, write_f, precision=maximum_precision)
    grad_wr = jnp.einsum("hkvt,kvn->ktn", weighted, read_function, precision=maximum_precision)
    grad_wr = grad_wr + jnp.einsum("hkt,khpn,kthp->ktn", to_end, leaving, values, precision=maximum_precision)
    grad_rd = jnp.einsum("hktu,kun->ktn", weighted, write_f, precision=maximum_precision)
    grad_rd = grad_rd + jnp.einsum("hkt,khpn,kthp->ktn", since_beginning, entering, gradient_function, precision=maximum_precision)
    return (mixer.reshape(length, per_group, HEAD_DIM), grad_in.reshape(length, per_group, HEAD_DIM),
            grad_wr.reshape(length, STATE), grad_rd.reshape(length, STATE))


def reference(head_input, write_vectors, read_vectors, log_decay, cotangent, out_weight, scale_exponent):
    per_group = HEADS // GROUPS
    scales = jnp.exp2(scale_exponent.astype(jnp.float32))
    dequantized = (out_weight.astype(jnp.float32) * jnp.repeat(scales, SCALE_BLOCK, axis=0)).astype(jnp.bfloat16)
    length = head_input.shape[1]
    columns = HEADS * HEAD_DIM

    def per_sequence(carry, pieces):
        cot_rows, input_rows, write_rows, read_rows, log_rows = pieces
        grad_mixer = jnp.dot(cot_rows, dequantized, preferred_element_type=jnp.float32).astype(jnp.bfloat16)
        grouped_in = jnp.transpose(input_rows.reshape(length, GROUPS, per_group, HEAD_DIM), (1, 0, 2, 3))
        grouped_grad = jnp.transpose(grad_mixer.reshape(length, GROUPS, per_group, HEAD_DIM), (1, 0, 2, 3))
        grouped_wr = jnp.transpose(write_rows.reshape(length, GROUPS, STATE), (1, 0, 2))
        grouped_rd = jnp.transpose(read_rows.reshape(length, GROUPS, STATE), (1, 0, 2))
        grouped_log = log_rows.reshape(GROUPS, per_group, length)
        mixer, grad_in, grad_wr, grad_rd = lax.map(lambda items: group_pass(*items),
                                                   (grouped_in, grouped_wr, grouped_rd, grouped_log, grouped_grad))
        mixer_out = jnp.transpose(mixer, (1, 0, 2, 3)).reshape(length, columns).astype(jnp.bfloat16)
        grad_in = jnp.transpose(grad_in, (1, 0, 2, 3)).reshape(length, columns).astype(jnp.bfloat16)
        grad_wr = jnp.transpose(grad_wr, (1, 0, 2)).reshape(length, GROUPS * STATE).astype(jnp.bfloat16)
        grad_rd = jnp.transpose(grad_rd, (1, 0, 2)).reshape(length, GROUPS * STATE).astype(jnp.bfloat16)
        update = lax.dot_general(cot_rows, mixer_out, (((0,), (0,)), ((), ())), preferred_element_type=jnp.float32)
        return carry + update, (grad_in, grad_wr, grad_rd)

    start_grad = jnp.zeros((D, columns), jnp.float32)
    grad_weight, stacked = lax.scan(per_sequence, start_grad,
                                    (cotangent, head_input, write_vectors, read_vectors, log_decay))
    return stacked[0], stacked[1], stacked[2], grad_weight
```

```python
import functools

import jax
import jax.numpy as jnp
from jax import lax
from jax.experimental import pallas as pl
from jax.experimental.pallas import tpu as pltpu
from jax.sharding import PartitionSpec as P

HEADS = 64
GROUPS = 4
HEAD_DIM = 64
STATE = 128
SCALE_BLOCK = 32
LANES = 128
VMEM_LIMIT = 50 * 1024 * 1024

bf16 = jnp.bfloat16
f32 = jnp.float32
HIGHEST = lax.Precision.HIGHEST


def call(kernel, out_shape, n_in, flops=0, bytes_accessed=0, scratch=(), in_specs=None):
    out_specs = jax.tree.map(lambda _: pl.BlockSpec(memory_space=pltpu.VMEM), out_shape)
    return pl.pallas_call(
        kernel,
        out_shape=out_shape,
        in_specs=in_specs or [pl.BlockSpec(memory_space=pltpu.VMEM)] * n_in,
        out_specs=out_specs,
        scratch_shapes=list(scratch),
        compiler_params=pltpu.CompilerParams(vmem_limit_bytes=VMEM_LIMIT),
        cost_estimate=pl.CostEstimate(
            flops=flops, bytes_accessed=bytes_accessed, transcendentals=0
        ),
    )


def dot(a, b, contract, precision=None):
    return lax.dot_general(
        a, b, ((contract[:1], contract[1:]), ((), ())),
        precision=precision, preferred_element_type=f32,
    )


def low_half(rows):
    return lax.broadcasted_iota(jnp.int32, (rows, LANES), 1) < HEAD_DIM


def pair_scale(columns, pair, rows):
    first = columns[:, 2 * pair : 2 * pair + 1]
    second = columns[:, 2 * pair + 1 : 2 * pair + 2]
    return jnp.where(low_half(rows), first, second)


def spread_matrix(heads):
    head = lax.broadcasted_iota(jnp.int32, (LANES, heads * HEAD_DIM), 0)
    column = lax.broadcasted_iota(jnp.int32, (LANES, heads * HEAD_DIM), 1)
    return jnp.where(column // HEAD_DIM == head, 1.0, 0.0).astype(f32)


def state_kernel(x_ref, w_ref, decay_ref, packed_ref, rows_ref, columns_ref):
    length, columns = x_ref.shape
    heads = decay_ref.shape[0]
    log_decay = decay_ref[...]
    row = lax.broadcasted_iota(jnp.int32, (length, length), 0)
    column = lax.broadcasted_iota(jnp.int32, (length, length), 1)
    upto = jnp.where(row <= column, 1.0, 0.0).astype(f32)
    cumulative = dot(log_decay, upto, (1, 0), HIGHEST)
    rows_ref[...] = cumulative
    padded = jnp.concatenate(
        [cumulative, jnp.zeros((LANES - heads, length), f32)], axis=0
    )
    turned = jnp.transpose(padded)
    columns_ref[...] = turned
    ends = turned[length - 1 : length, :]
    to_end = jnp.exp(ends - turned)
    w = w_ref[...]
    for pair in range(heads // 2):
        lanes = slice(pair * LANES, (pair + 1) * LANES)
        scaled = x_ref[:, lanes].astype(f32) * pair_scale(to_end, pair, length)
        packed_ref[:, lanes] = dot(w, scaled.astype(bf16), (0, 0)).astype(bf16)
    high = ends.astype(bf16).astype(f32)
    middle = (ends - high).astype(bf16).astype(f32)
    low = ends - high - middle
    which = lax.broadcasted_iota(jnp.int32, (STATE, LANES), 0) % 8
    terms = jnp.where(
        which == 0, high, jnp.where(which == 1, middle, jnp.where(which == 2, low, 0.0))
    )
    packed_ref[:, columns:] = terms.astype(bf16)


def forward_scan_kernel(packed_ref, entering_ref, decay_ref):
    rows, total = packed_ref.shape
    columns = entering_ref.shape[1]
    size = decay_ref.shape[0]
    chunk = rows // size
    everything = packed_ref[...].astype(f32)
    terms = everything[:, columns:]
    sums = [
        jnp.sum(terms[k * chunk : (k + 1) * chunk], axis=0, keepdims=True) for k in range(size)
    ]
    decays = jnp.exp(jnp.concatenate(sums, axis=0))
    spread = dot(decays, spread_matrix(columns // HEAD_DIM), (1, 0), HIGHEST)
    decay_ref[...] = spread
    carry = jnp.zeros((chunk, columns), f32)
    before = []
    for k in range(size):
        before.append(carry)
        carry = spread[k : k + 1] * carry + everything[k * chunk : (k + 1) * chunk, :columns]
    entering_ref[...] = jnp.concatenate(before, axis=0).astype(bf16)


def backward_scan_kernel(summary_ref, decay_ref, leaving_ref):
    rows, columns = summary_ref.shape
    size = decay_ref.shape[0]
    chunk = rows // size
    everything = summary_ref[...].astype(f32)
    spread = decay_ref[...]
    carry = jnp.zeros((chunk, columns), f32)
    after = [None] * size
    for k in range(size - 1, -1, -1):
        after[k] = carry
        carry = spread[k : k + 1] * carry + everything[k * chunk : (k + 1) * chunk]
    leaving_ref[...] = jnp.concatenate(after, axis=0).astype(bf16)


def mixer_kernel(x_ref, w_ref, r_ref, rows_ref, columns_ref, entering_ref, out_ref):
    length = x_ref.shape[0]
    heads = rows_ref.shape[0]
    r = r_ref[...]
    row = lax.broadcasted_iota(jnp.int32, (length, length), 0)
    column = lax.broadcasted_iota(jnp.int32, (length, length), 1)
    meets = jnp.where(row >= column, dot(r, w_ref[...], (1, 1)), 0.0)
    cumulative = columns_ref[...]
    since = jnp.exp(cumulative)
    half = low_half(length)
    for pair in range(heads // 2):
        lanes = slice(pair * LANES, (pair + 1) * LANES)
        x = x_ref[:, lanes]
        parts = []
        for head in (2 * pair, 2 * pair + 1):
            difference = cumulative[:, head : head + 1] - rows_ref[head : head + 1, :]
            mixing = jnp.exp(jnp.minimum(difference, 0.0)) * meets
            parts.append(dot(mixing.astype(bf16), x, (1, 0)))
        carried = dot(r, entering_ref[:, lanes], (1, 0)) * pair_scale(since, pair, length)
        out_ref[:, lanes] = (jnp.where(half, parts[0], parts[1]) + carried).astype(bf16)


def project_kernel(place_ref, c0, c1, c2, c3, weight_ref, o0, o1, o2, o3, held, sems):
    copies = []
    for m, ref in enumerate((c0, c1, c2, c3)):
        slot = lax.rem(place_ref[0] + 8 - m, 4)
        copy = pltpu.make_async_copy(ref, held.at[slot], sems.at[m])
        copy.start()
        copies.append(copy)
    for copy in copies:
        copy.wait()
    weight = weight_ref[...]
    for n, out in enumerate((o0, o1, o2, o3)):
        out[...] = dot(held[n], weight, (1, 0)).astype(bf16)


def adjoint_kernel(g0, g1, g2, g3, r_ref, columns_ref, grad_ref, summary_ref):
    length, columns = g0.shape
    heads = columns // HEAD_DIM
    since = jnp.exp(columns_ref[...])
    r = r_ref[...]
    for pair in range(heads // 2):
        lanes = slice(pair * LANES, (pair + 1) * LANES)
        total = (g0[:, lanes].astype(f32) + g1[:, lanes].astype(f32)) + (
            g2[:, lanes].astype(f32) + g3[:, lanes].astype(f32)
        )
        grad = total.astype(bf16)
        grad_ref[:, lanes] = grad
        scaled = grad.astype(f32) * pair_scale(since, pair, length)
        summary_ref[:, lanes] = dot(r, scaled.astype(bf16), (0, 0)).astype(bf16)


def gradients_kernel(
    x_ref, w_ref, r_ref, g_ref, rows_ref, columns_ref, entering_ref, leaving_ref,
    grad_input_ref, grad_write_ref, grad_read_ref,
):
    length = x_ref.shape[0]
    heads = rows_ref.shape[0]
    w = w_ref[...]
    r = r_ref[...]
    row = lax.broadcasted_iota(jnp.int32, (length, length), 0)
    column = lax.broadcasted_iota(jnp.int32, (length, length), 1)
    later = column >= row
    meets = jnp.where(later, dot(w, r, (1, 1)), 0.0)
    cumulative = columns_ref[...]
    since = jnp.exp(cumulative)
    to_end = jnp.exp(cumulative[length - 1 : length, :] - cumulative)
    half = low_half(length)
    weighted = jnp.zeros((length, length), f32)
    grad_write = jnp.zeros((length, STATE), f32)
    grad_read = jnp.zeros((length, STATE), f32)
    for pair in range(heads // 2):
        lanes = slice(pair * LANES, (pair + 1) * LANES)
        x = x_ref[:, lanes]
        g = g_ref[:, lanes]
        parts = []
        for head in (2 * pair, 2 * pair + 1):
            difference = rows_ref[head : head + 1, :] - cumulative[:, head : head + 1]
            within = jnp.exp(jnp.minimum(difference, 0.0))
            parts.append(dot((within * meets).astype(bf16), g, (1, 0)))
            mine = half if head % 2 == 0 else jnp.logical_not(half)
            own = jnp.where(mine, x, jnp.zeros_like(x))
            weighted = weighted + within * dot(own, g, (1, 1))
        end_scale = pair_scale(to_end, pair, length)
        leaving = leaving_ref[:, lanes]
        carried = dot(w, leaving, (1, 0)) * end_scale
        grad_input_ref[:, lanes] = (jnp.where(half, parts[0], parts[1]) + carried).astype(bf16)
        grad_write += dot((x.astype(f32) * end_scale).astype(bf16), leaving, (1, 1))
        scaled = (g.astype(f32) * pair_scale(since, pair, length)).astype(bf16)
        grad_read += dot(scaled, entering_ref[:, lanes], (1, 1))
    weighted = jnp.where(later, weighted, 0.0).astype(bf16)
    grad_write_ref[...] = (grad_write + dot(weighted, r, (1, 0))).astype(bf16)
    grad_read_ref[...] = (grad_read + dot(weighted, w, (0, 0))).astype(bf16)


def weight_kernel(
    place_ref, c0, c1, c2, c3, m0, m1, m2, m3, mine_ref, other_ref, held, total, sems
):
    copies = []
    for m, ref in enumerate((c0, c1, c2, c3)):
        slot = lax.rem(place_ref[0] + 8 - m, 4)
        copy = pltpu.make_async_copy(ref, held.at[slot], sems.at[m])
        copy.start()
        copies.append(copy)
    for copy in copies:
        copy.wait()
    mixers = (m0, m3, m2, m1)
    acc = dot(held[0], mixers[0][...], (0, 0))
    for n in range(1, 4):
        acc = acc + dot(held[n], mixers[n][...], (0, 0))
    total[...] = acc
    ring, rows = mine_ref.shape[0], mine_ref.shape[1]
    z, core = place_ref[1], place_ref[2]
    for n in range(ring):
        target = 2 * lax.rem(z + n, ring)
        start = pl.multiple_of((target + core) * rows, rows)
        mine_ref[n] = total[pl.ds(start, rows), :].astype(bf16)
        start = pl.multiple_of((target + 1 - core) * rows, rows)
        other_ref[n] = total[pl.ds(start, rows), :].astype(bf16)


def add_kernel(mine_ref, other_ref, *outs):
    for n, out in enumerate(outs):
        out[...] = (mine_ref[n].astype(f32) + other_ref[n].astype(f32)).astype(out.dtype)


def sum_kernel(own_ref, *refs):
    *parts, out_ref = refs
    total = own_ref[...].astype(f32)
    for part in parts:
        total = total + part[...].astype(f32)
    out_ref[...] = total


def shape(dims, dtype=bf16):
    return jax.ShapeDtypeStruct(dims, dtype)


def per_device(
    head_input, write_vectors, read_vectors, log_decay, cotangent, out_weight, scale_exponent
):
    dp, ctx, tp = (lax.axis_size(name) for name in ("dp", "ctx", "tp"))
    ring = ctx // 2
    mine_dp, mine_ctx, mine_tp = (lax.axis_index(name) for name in ("dp", "ctx", "tp"))
    x, w, r = head_input[0], write_vectors[0], read_vectors[0]
    length, columns = x.shape
    heads = log_decay.shape[1]
    place = jnp.stack(
        [mine_tp - mine_dp + dp, mine_ctx // 2, lax.rem(mine_ctx, 2)]
    ).astype(jnp.int32)

    def across(value, m):
        pairs = [
            (a * tp + k, k * tp + (a + m) % tp) for a in range(dp) for k in range(tp)
        ]
        return lax.ppermute(value, ("dp", "tp"), pairs)

    def along_dp(value, n):
        return lax.ppermute(value, "dp", [(i, (i + n) % dp) for i in range(dp)])

    def along_z(value, n):
        return lax.ppermute(value, "ctx", [(i, (i + 2 * n) % ctx) for i in range(ctx)])

    def other_core(value):
        return lax.ppermute(value, "ctx", [(i, i ^ 1) for i in range(ctx)])

    cots = [across(cotangent[0], m) for m in range(tp)]
    scales = jnp.exp2(scale_exponent.astype(f32))
    dequant = (out_weight.astype(f32) * jnp.repeat(scales, SCALE_BLOCK, axis=0)).astype(bf16)
    weight = lax.all_gather(dequant, "ctx", axis=0, tiled=True)

    packed, cum_rows, cum_columns = call(
        state_kernel,
        [shape((STATE, columns + LANES)), shape((heads, length), f32), shape((length, LANES), f32)],
        3,
    )(x, w, log_decay[0])
    packed = lax.all_to_all(packed, "ctx", 0, 0, tiled=True)
    entering, decays = call(
        forward_scan_kernel, [shape((STATE, columns)), shape((ctx, columns), f32)], 1
    )(packed)
    entering = lax.all_to_all(entering, "ctx", 0, 0, tiled=True)
    mixer = call(mixer_kernel, shape((length, columns)), 6)(
        x, w, r, cum_rows, cum_columns, entering
    )
    mixers = [mixer] + [along_dp(mixer, n) for n in range(1, dp)]

    smem = pl.BlockSpec(memory_space=pltpu.SMEM)
    vmem = pl.BlockSpec(memory_space=pltpu.VMEM)
    anywhere = pl.BlockSpec(memory_space=pl.ANY)
    model = cotangent.shape[2]
    parts = call(
        project_kernel,
        [shape((length, columns))] * dp,
        6,
        scratch=[pltpu.VMEM((dp, length, model), bf16), pltpu.SemaphoreType.DMA((dp,))],
        in_specs=[smem] + [anywhere] * dp + [vmem],
    )(place, *cots, weight)
    arrived = [along_dp(parts[n], n) for n in range(1, dp)]
    grad, summary = call(adjoint_kernel, [shape((length, columns)), shape((STATE, columns))], 6)(
        parts[0], *arrived, r, cum_columns
    )
    summary = lax.all_to_all(summary, "ctx", 0, 0, tiled=True)
    leaving = call(backward_scan_kernel, shape((STATE, columns)), 2)(summary, decays)
    leaving = lax.all_to_all(leaving, "ctx", 0, 0, tiled=True)

    rows = model // ctx
    mine, other = call(
        weight_kernel,
        [shape((ring, rows, columns))] * 2,
        9,
        scratch=[
            pltpu.VMEM((dp, length, model), bf16),
            pltpu.VMEM((model, columns), f32),
            pltpu.SemaphoreType.DMA((dp,)),
        ],
        in_specs=[smem] + [anywhere] * dp + [vmem] * dp,
    )(place, *cots, *mixers)
    other = other_core(other)
    blocks = call(add_kernel, [shape((rows, columns))] * ring, 2)(mine, other)
    received = [along_z(blocks[n], n) for n in range(1, ring)]
    grad_weight = call(sum_kernel, shape((rows, columns), f32), ring)(blocks[0], *received)

    grad_input, grad_write, grad_read = call(
        gradients_kernel,
        [shape((length, columns)), shape((length, STATE)), shape((length, STATE))],
        8,
    )(x, w, r, grad, cum_rows, cum_columns, entering, leaving)
    return grad_input[None], grad_write[None], grad_read[None], grad_weight


def solution(mesh):
    return jax.shard_map(
        per_device,
        mesh=mesh,
        in_specs=(
            P("dp", "ctx", "tp"),
            P("dp", "ctx", "tp"),
            P("dp", "ctx", "tp"),
            P("dp", "tp", "ctx"),
            P("dp", "ctx", "tp"),
            P(("dp", "ctx"), "tp"),
            P(("dp", "ctx"), "tp"),
        ),
        out_specs=(
            P("dp", "ctx", "tp"),
            P("dp", "ctx", "tp"),
            P("dp", "ctx", "tp"),
            P(("dp", "ctx"), "tp"),
        ),
        check_vma=False,
    )
```

```python
import functools

import jax
import jax.numpy as jnp
from jax import lax
from jax.experimental import pallas as pl
from jax.experimental.pallas import tpu as pltpu
from jax.sharding import PartitionSpec as P

HEADS = 64
GROUPS = 4
HEAD_DIM = 64
STATE = 128
SCALE_BLOCK = 32
LANES = 128
VMEM_LIMIT = 50 * 1024 * 1024

bf16 = jnp.bfloat16
f32 = jnp.float32
HIGHEST = lax.Precision.HIGHEST


def call(kernel, out_shape, n_in, flops=0, bytes_accessed=0, scratch=(), in_specs=None):
    out_specs = jax.tree.map(lambda _: pl.BlockSpec(memory_space=pltpu.VMEM), out_shape)
    return pl.pallas_call(
        kernel,
        out_shape=out_shape,
        in_specs=in_specs or [pl.BlockSpec(memory_space=pltpu.VMEM)] * n_in,
        out_specs=out_specs,
        scratch_shapes=list(scratch),
        compiler_params=pltpu.CompilerParams(vmem_limit_bytes=VMEM_LIMIT),
        cost_estimate=pl.CostEstimate(
            flops=flops, bytes_accessed=bytes_accessed, transcendentals=0
        ),
    )


def dot(a, b, contract, precision=None):
    return lax.dot_general(
        a, b, ((contract[:1], contract[1:]), ((), ())),
        precision=precision, preferred_element_type=f32,
    )


def low_half(rows):
    return lax.broadcasted_iota(jnp.int32, (rows, LANES), 1) < HEAD_DIM


def pair_scale(columns, pair, rows):
    first = columns[:, 2 * pair : 2 * pair + 1]
    second = columns[:, 2 * pair + 1 : 2 * pair + 2]
    return jnp.where(low_half(rows), first, second)


def spread_matrix(heads):
    head = lax.broadcasted_iota(jnp.int32, (LANES, heads * HEAD_DIM), 0)
    column = lax.broadcasted_iota(jnp.int32, (LANES, heads * HEAD_DIM), 1)
    return jnp.where(column // HEAD_DIM == head, 1.0, 0.0).astype(f32)


def dequant_kernel(weight_ref, exponent_ref, out_ref):
    scales = jnp.exp2(exponent_ref[...].astype(f32))
    for block in range(scales.shape[0]):
        rows = slice(block * SCALE_BLOCK, (block + 1) * SCALE_BLOCK)
        out_ref[rows, :] = (
            weight_ref[rows, :].astype(f32) * scales[block : block + 1, :]
        ).astype(bf16)


def state_kernel(x_ref, w_ref, decay_ref, packed_ref, rows_ref, columns_ref):
    length, columns = x_ref.shape
    heads = decay_ref.shape[0]
    log_decay = decay_ref[...]
    row = lax.broadcasted_iota(jnp.int32, (length, length), 0)
    column = lax.broadcasted_iota(jnp.int32, (length, length), 1)
    upto = jnp.where(row <= column, 1.0, 0.0).astype(f32)
    cumulative = dot(log_decay, upto, (1, 0), HIGHEST)
    rows_ref[...] = cumulative
    padded = jnp.concatenate(
        [cumulative, jnp.zeros((LANES - heads, length), f32)], axis=0
    )
    turned = jnp.transpose(padded)
    columns_ref[...] = turned
    ends = turned[length - 1 : length, :]
    to_end = jnp.exp(ends - turned)
    w = w_ref[...]
    for pair in range(heads // 2):
        lanes = slice(pair * LANES, (pair + 1) * LANES)
        scaled = x_ref[:, lanes].astype(f32) * pair_scale(to_end, pair, length)
        packed_ref[:, lanes] = dot(w, scaled.astype(bf16), (0, 0)).astype(bf16)
    high = ends.astype(bf16).astype(f32)
    middle = (ends - high).astype(bf16).astype(f32)
    low = ends - high - middle
    which = lax.broadcasted_iota(jnp.int32, (STATE, LANES), 0) % 8
    terms = jnp.where(
        which == 0, high, jnp.where(which == 1, middle, jnp.where(which == 2, low, 0.0))
    )
    packed_ref[:, columns:] = terms.astype(bf16)


def forward_scan_kernel(packed_ref, entering_ref, decay_ref):
    rows, total = packed_ref.shape
    columns = entering_ref.shape[1]
    size = decay_ref.shape[0]
    chunk = rows // size
    everything = packed_ref[...].astype(f32)
    terms = everything[:, columns:]
    sums = [
        jnp.sum(terms[k * chunk : (k + 1) * chunk], axis=0, keepdims=True) for k in range(size)
    ]
    decays = jnp.exp(jnp.concatenate(sums, axis=0))
    spread = dot(decays, spread_matrix(columns // HEAD_DIM), (1, 0), HIGHEST)
    decay_ref[...] = spread
    carry = jnp.zeros((chunk, columns), f32)
    before = []
    for k in range(size):
        before.append(carry)
        carry = spread[k : k + 1] * carry + everything[k * chunk : (k + 1) * chunk, :columns]
    entering_ref[...] = jnp.concatenate(before, axis=0).astype(bf16)


def backward_scan_kernel(summary_ref, decay_ref, leaving_ref):
    rows, columns = summary_ref.shape
    size = decay_ref.shape[0]
    chunk = rows // size
    everything = summary_ref[...].astype(f32)
    spread = decay_ref[...]
    carry = jnp.zeros((chunk, columns), f32)
    after = [None] * size
    for k in range(size - 1, -1, -1):
        after[k] = carry
        carry = spread[k : k + 1] * carry + everything[k * chunk : (k + 1) * chunk]
    leaving_ref[...] = jnp.concatenate(after, axis=0).astype(bf16)


def mixer_kernel(x_ref, w_ref, r_ref, rows_ref, columns_ref, entering_ref, out_ref):
    length = x_ref.shape[0]
    heads = rows_ref.shape[0]
    r = r_ref[...]
    row = lax.broadcasted_iota(jnp.int32, (length, length), 0)
    column = lax.broadcasted_iota(jnp.int32, (length, length), 1)
    meets = jnp.where(row >= column, dot(r, w_ref[...], (1, 1)), 0.0)
    cumulative = columns_ref[...]
    since = jnp.exp(cumulative)
    half = low_half(length)
    for pair in range(heads // 2):
        lanes = slice(pair * LANES, (pair + 1) * LANES)
        x = x_ref[:, lanes]
        parts = []
        for head in (2 * pair, 2 * pair + 1):
            difference = cumulative[:, head : head + 1] - rows_ref[head : head + 1, :]
            mixing = jnp.exp(jnp.minimum(difference, 0.0)) * meets
            parts.append(dot(mixing.astype(bf16), x, (1, 0)))
        carried = dot(r, entering_ref[:, lanes], (1, 0)) * pair_scale(since, pair, length)
        out_ref[:, lanes] = (jnp.where(half, parts[0], parts[1]) + carried).astype(bf16)


def project_kernel(c0, c1, c2, c3, weight_ref, o0, o1, o2, o3, held, sems):
    copies = []
    for m, ref in enumerate((c0, c1, c2, c3)):
        slot = lax.rem(lax.axis_index("tp") - lax.axis_index("dp") + 8 - m, 4)
        copy = pltpu.make_async_copy(ref, held.at[slot], sems.at[m])
        copy.start()
        copies.append(copy)
    for copy in copies:
        copy.wait()
    weight = weight_ref[...]
    for n, out in enumerate((o0, o1, o2, o3)):
        out[...] = dot(held[n], weight, (1, 0)).astype(bf16)


def adjoint_kernel(g0, g1, g2, g3, r_ref, columns_ref, grad_ref, summary_ref):
    length, columns = g0.shape
    heads = columns // HEAD_DIM
    since = jnp.exp(columns_ref[...])
    r = r_ref[...]
    for pair in range(heads // 2):
        lanes = slice(pair * LANES, (pair + 1) * LANES)
        total = (g0[:, lanes].astype(f32) + g1[:, lanes].astype(f32)) + (
            g2[:, lanes].astype(f32) + g3[:, lanes].astype(f32)
        )
        grad = total.astype(bf16)
        grad_ref[:, lanes] = grad
        scaled = grad.astype(f32) * pair_scale(since, pair, length)
        summary_ref[:, lanes] = dot(r, scaled.astype(bf16), (0, 0)).astype(bf16)


def gradients_kernel(
    x_ref, w_ref, r_ref, g_ref, rows_ref, columns_ref, entering_ref, leaving_ref,
    grad_input_ref, grad_write_ref, grad_read_ref,
):
    length = x_ref.shape[0]
    heads = rows_ref.shape[0]
    w = w_ref[...]
    r = r_ref[...]
    row = lax.broadcasted_iota(jnp.int32, (length, length), 0)
    column = lax.broadcasted_iota(jnp.int32, (length, length), 1)
    later = column >= row
    meets = jnp.where(later, dot(w, r, (1, 1)), 0.0)
    cumulative = columns_ref[...]
    since = jnp.exp(cumulative)
    to_end = jnp.exp(cumulative[length - 1 : length, :] - cumulative)
    half = low_half(length)
    weighted = jnp.zeros((length, length), f32)
    grad_write = jnp.zeros((length, STATE), f32)
    grad_read = jnp.zeros((length, STATE), f32)
    for pair in range(heads // 2):
        lanes = slice(pair * LANES, (pair + 1) * LANES)
        x = x_ref[:, lanes]
        g = g_ref[:, lanes]
        parts = []
        for head in (2 * pair, 2 * pair + 1):
            difference = rows_ref[head : head + 1, :] - cumulative[:, head : head + 1]
            within = jnp.exp(jnp.minimum(difference, 0.0))
            parts.append(dot((within * meets).astype(bf16), g, (1, 0)))
            mine = half if head % 2 == 0 else jnp.logical_not(half)
            own = jnp.where(mine, x, jnp.zeros_like(x))
            weighted = weighted + within * dot(own, g, (1, 1))
        end_scale = pair_scale(to_end, pair, length)
        leaving = leaving_ref[:, lanes]
        carried = dot(w, leaving, (1, 0)) * end_scale
        grad_input_ref[:, lanes] = (jnp.where(half, parts[0], parts[1]) + carried).astype(bf16)
        grad_write += dot((x.astype(f32) * end_scale).astype(bf16), leaving, (1, 1))
        scaled = (g.astype(f32) * pair_scale(since, pair, length)).astype(bf16)
        grad_read += dot(scaled, entering_ref[:, lanes], (1, 1))
    weighted = jnp.where(later, weighted, 0.0).astype(bf16)
    grad_write_ref[...] = (grad_write + dot(weighted, r, (1, 0))).astype(bf16)
    grad_read_ref[...] = (grad_read + dot(weighted, w, (0, 0))).astype(bf16)


def weight_kernel(
    c0, c1, c2, c3, m0, m1, m2, m3, out_ref, held, sems
):
    copies = []
    for m, ref in enumerate((c0, c1, c2, c3)):
        slot = lax.rem(lax.axis_index("tp") - lax.axis_index("dp") + 8 - m, 4)
        copy = pltpu.make_async_copy(ref, held.at[slot], sems.at[m])
        copy.start()
        copies.append(copy)
    for copy in copies:
        copy.wait()
    mixers = (m0, m3, m2, m1)
    acc = dot(held[0], mixers[0][...], (0, 0))
    for n in range(1, 4):
        acc = acc + dot(held[n], mixers[n][...], (0, 0))
    out_ref[...] = acc


def shape(dims, dtype=bf16):
    return jax.ShapeDtypeStruct(dims, dtype)


def per_device(
    head_input, write_vectors, read_vectors, log_decay, cotangent, out_weight, scale_exponent
):
    dp, ctx, tp = (lax.axis_size(name) for name in ("dp", "ctx", "tp"))
    x, w, r = head_input[0], write_vectors[0], read_vectors[0]
    length, columns = x.shape
    heads = log_decay.shape[1]

    def transposed(value):
        pairs = [(a * tp + k, k * tp + a) for a in range(dp) for k in range(tp)]
        return lax.ppermute(value, ("dp", "tp"), pairs)

    def along_tp(value, n):
        return lax.ppermute(value, "tp", [(i, (i + n) % tp) for i in range(tp)])

    def along_dp(value, n):
        return lax.ppermute(value, "dp", [(i, (i + n) % dp) for i in range(dp)])

    turned = transposed(cotangent[0])
    cots = [turned] + [along_tp(turned, m) for m in range(1, tp)]
    dequant = call(dequant_kernel, shape(out_weight.shape), 2)(out_weight, scale_exponent)
    weight = lax.all_gather(dequant, "ctx", axis=0, tiled=True)

    packed, cum_rows, cum_columns = call(
        state_kernel,
        [shape((STATE, columns + LANES)), shape((heads, length), f32), shape((length, LANES), f32)],
        3,
    )(x, w, log_decay[0])
    packed = lax.all_to_all(packed, "ctx", 0, 0, tiled=True)
    entering, decays = call(
        forward_scan_kernel, [shape((STATE, columns)), shape((ctx, columns), f32)], 1
    )(packed)
    entering = lax.all_to_all(entering, "ctx", 0, 0, tiled=True)

    mixer = call(mixer_kernel, shape((length, columns)), 6)(
        x, w, r, cum_rows, cum_columns, entering
    )
    mixer, weight = lax.optimization_barrier((mixer, weight))
    mixers = [mixer] + [along_dp(mixer, n) for n in range(1, dp)]

    vmem = pl.BlockSpec(memory_space=pltpu.VMEM)
    anywhere = pl.BlockSpec(memory_space=pl.ANY)
    model = cotangent.shape[2]
    parts = call(
        project_kernel,
        [shape((length, columns))] * dp,
        5,
        scratch=[pltpu.VMEM((dp, length, model), bf16), pltpu.SemaphoreType.DMA((dp,))],
        in_specs=[anywhere] * dp + [vmem],
    )(*cots, weight)
    arrived = [along_dp(parts[n], n) for n in range(1, dp)]

    parts, mixers = lax.optimization_barrier((parts, mixers))
    total = call(
        weight_kernel,
        shape((model, columns), f32),
        8,
        scratch=[pltpu.VMEM((dp, length, model), bf16), pltpu.SemaphoreType.DMA((dp,))],
        in_specs=[anywhere] * dp + [vmem] * dp,
    )(*cots, *mixers)
    grad_weight = lax.psum_scatter(total, "ctx", scatter_dimension=0, tiled=True)
    grad, summary = call(adjoint_kernel, [shape((length, columns)), shape((STATE, columns))], 6)(
        parts[0], *arrived, r, cum_columns
    )
    summary = lax.all_to_all(summary, "ctx", 0, 0, tiled=True)
    leaving = call(backward_scan_kernel, shape((STATE, columns)), 2)(summary, decays)
    leaving = lax.all_to_all(leaving, "ctx", 0, 0, tiled=True)
    grad_input, grad_write, grad_read = call(
        gradients_kernel,
        [shape((length, columns)), shape((length, STATE)), shape((length, STATE))],
        8,
    )(x, w, r, grad, cum_rows, cum_columns, entering, leaving)
    return grad_input[None], grad_write[None], grad_read[None], grad_weight


def solution(mesh):
    return jax.shard_map(
        per_device,
        mesh=mesh,
        in_specs=(
            P("dp", "ctx", "tp"),
            P("dp", "ctx", "tp"),
            P("dp", "ctx", "tp"),
            P("dp", "tp", "ctx"),
            P("dp", "ctx", "tp"),
            P(("dp", "ctx"), "tp"),
            P(("dp", "ctx"), "tp"),
        ),
        out_specs=(
            P("dp", "ctx", "tp"),
            P("dp", "ctx", "tp"),
            P("dp", "ctx", "tp"),
            P(("dp", "ctx"), "tp"),
        ),
        check_vma=False,
    )
```

```python
import functools

import jax
import jax.numpy as jnp
from jax import lax
from jax.experimental import pallas as pl
from jax.experimental.pallas import tpu as pltpu
from jax.sharding import PartitionSpec as P

HEADS = 64
GROUPS = 4
HEAD_DIM = 64
STATE = 128
SCALE_BLOCK = 32
LANES = 128
VMEM_LIMIT = 50 * 1024 * 1024

bf16 = jnp.bfloat16
f32 = jnp.float32
HIGHEST = lax.Precision.HIGHEST


def call(kernel, out_shape, n_in, flops=0, bytes_accessed=0, scratch=(), in_specs=None):
    out_specs = jax.tree.map(lambda _: pl.BlockSpec(memory_space=pltpu.VMEM), out_shape)
    return pl.pallas_call(
        kernel,
        out_shape=out_shape,
        in_specs=in_specs or [pl.BlockSpec(memory_space=pltpu.VMEM)] * n_in,
        out_specs=out_specs,
        scratch_shapes=list(scratch),
        compiler_params=pltpu.CompilerParams(vmem_limit_bytes=VMEM_LIMIT),
        cost_estimate=pl.CostEstimate(
            flops=flops, bytes_accessed=bytes_accessed, transcendentals=0
        ),
    )


def dot(a, b, contract, precision=None):
    return lax.dot_general(
        a, b, ((contract[:1], contract[1:]), ((), ())),
        precision=precision, preferred_element_type=f32,
    )


def low_half(rows):
    return lax.broadcasted_iota(jnp.int32, (rows, LANES), 1) < HEAD_DIM


def pair_scale(columns, pair, rows):
    first = columns[:, 2 * pair : 2 * pair + 1]
    second = columns[:, 2 * pair + 1 : 2 * pair + 2]
    return jnp.where(low_half(rows), first, second)


def spread_matrix(heads):
    head = lax.broadcasted_iota(jnp.int32, (LANES, heads * HEAD_DIM), 0)
    column = lax.broadcasted_iota(jnp.int32, (LANES, heads * HEAD_DIM), 1)
    return jnp.where(column // HEAD_DIM == head, 1.0, 0.0).astype(f32)


def dequant_kernel(weight_ref, exponent_ref, out_ref):
    scales = jnp.exp2(exponent_ref[...].astype(f32))
    for block in range(scales.shape[0]):
        rows = slice(block * SCALE_BLOCK, (block + 1) * SCALE_BLOCK)
        out_ref[rows, :] = (
            weight_ref[rows, :].astype(f32) * scales[block : block + 1, :]
        ).astype(bf16)


def state_kernel(x_ref, w_ref, decay_ref, packed_ref, rows_ref, columns_ref):
    length, columns = x_ref.shape
    heads = decay_ref.shape[0]
    log_decay = decay_ref[...]
    row = lax.broadcasted_iota(jnp.int32, (length, length), 0)
    column = lax.broadcasted_iota(jnp.int32, (length, length), 1)
    upto = jnp.where(row <= column, 1.0, 0.0).astype(f32)
    cumulative = dot(log_decay, upto, (1, 0), HIGHEST)
    rows_ref[...] = cumulative
    padded = jnp.concatenate(
        [cumulative, jnp.zeros((LANES - heads, length), f32)], axis=0
    )
    turned = jnp.transpose(padded)
    columns_ref[...] = turned
    ends = turned[length - 1 : length, :]
    to_end = jnp.exp(ends - turned)
    w = w_ref[...]
    for pair in range(heads // 2):
        lanes = slice(pair * LANES, (pair + 1) * LANES)
        scaled = x_ref[:, lanes].astype(f32) * pair_scale(to_end, pair, length)
        packed_ref[:, lanes] = dot(w, scaled.astype(bf16), (0, 0)).astype(bf16)
    high = ends.astype(bf16).astype(f32)
    middle = (ends - high).astype(bf16).astype(f32)
    low = ends - high - middle
    which = lax.broadcasted_iota(jnp.int32, (STATE, LANES), 0) % 8
    terms = jnp.where(
        which == 0, high, jnp.where(which == 1, middle, jnp.where(which == 2, low, 0.0))
    )
    packed_ref[:, columns:] = terms.astype(bf16)


def forward_scan_kernel(packed_ref, entering_ref, decay_ref):
    rows, total = packed_ref.shape
    columns = entering_ref.shape[1]
    size = decay_ref.shape[0]
    chunk = rows // size
    everything = packed_ref[...].astype(f32)
    terms = everything[:, columns:]
    sums = [
        jnp.sum(terms[k * chunk : (k + 1) * chunk], axis=0, keepdims=True) for k in range(size)
    ]
    decays = jnp.exp(jnp.concatenate(sums, axis=0))
    spread = dot(decays, spread_matrix(columns // HEAD_DIM), (1, 0), HIGHEST)
    decay_ref[...] = spread
    carry = jnp.zeros((chunk, columns), f32)
    before = []
    for k in range(size):
        before.append(carry)
        carry = spread[k : k + 1] * carry + everything[k * chunk : (k + 1) * chunk, :columns]
    entering_ref[...] = jnp.concatenate(before, axis=0).astype(bf16)


def backward_scan_kernel(summary_ref, decay_ref, leaving_ref):
    rows, columns = summary_ref.shape
    size = decay_ref.shape[0]
    chunk = rows // size
    everything = summary_ref[...].astype(f32)
    spread = decay_ref[...]
    carry = jnp.zeros((chunk, columns), f32)
    after = [None] * size
    for k in range(size - 1, -1, -1):
        after[k] = carry
        carry = spread[k : k + 1] * carry + everything[k * chunk : (k + 1) * chunk]
    leaving_ref[...] = jnp.concatenate(after, axis=0).astype(bf16)


def mixer_kernel(x_ref, w_ref, r_ref, rows_ref, columns_ref, entering_ref, out_ref):
    length = x_ref.shape[0]
    heads = rows_ref.shape[0]
    r = r_ref[...]
    row = lax.broadcasted_iota(jnp.int32, (length, length), 0)
    column = lax.broadcasted_iota(jnp.int32, (length, length), 1)
    meets = jnp.where(row >= column, dot(r, w_ref[...], (1, 1)), 0.0)
    cumulative = columns_ref[...]
    since = jnp.exp(cumulative)
    half = low_half(length)
    for pair in range(heads // 2):
        lanes = slice(pair * LANES, (pair + 1) * LANES)
        x = x_ref[:, lanes]
        parts = []
        for head in (2 * pair, 2 * pair + 1):
            difference = cumulative[:, head : head + 1] - rows_ref[head : head + 1, :]
            mixing = jnp.exp(jnp.minimum(difference, 0.0)) * meets
            parts.append(dot(mixing.astype(bf16), x, (1, 0)))
        carried = dot(r, entering_ref[:, lanes], (1, 0)) * pair_scale(since, pair, length)
        out_ref[:, lanes] = (jnp.where(half, parts[0], parts[1]) + carried).astype(bf16)


def project_kernel(c0, c1, c2, c3, weight_ref, o0, o1, o2, o3, o4, held, sems):
    copies = []
    for m, ref in enumerate((c0, c1, c2, c3)):
        slot = lax.rem(lax.axis_index("tp") - lax.axis_index("dp") + 8 - m, 4)
        copy = pltpu.make_async_copy(ref, held.at[slot], sems.at[m])
        copy.start()
        copies.append(copy)
    for copy in copies:
        copy.wait()
    weight = weight_ref[...]
    half = o3.shape[0]
    opposite = dot(held[2], weight, (1, 0)).astype(bf16)
    o3[...] = opposite[:half]
    o4[...] = opposite[half:]
    for n, out in ((1, o1), (3, o2), (0, o0)):
        out[...] = dot(held[n], weight, (1, 0)).astype(bf16)


def fold_kernel(p1, p2, top, bottom, o1, o2):
    half = top.shape[0]
    o1[:half, :] = (p1[:half, :].astype(f32) + top[...].astype(f32)).astype(bf16)
    o1[half:, :] = p1[half:, :]
    o2[:half, :] = p2[:half, :]
    o2[half:, :] = (p2[half:, :].astype(f32) + bottom[...].astype(f32)).astype(bf16)


def adjoint_kernel(g0, g1, g2, r_ref, columns_ref, grad_ref, summary_ref):
    length, columns = g0.shape
    heads = columns // HEAD_DIM
    since = jnp.exp(columns_ref[...])
    r = r_ref[...]
    for pair in range(heads // 2):
        lanes = slice(pair * LANES, (pair + 1) * LANES)
        total = g0[:, lanes].astype(f32) + g1[:, lanes].astype(f32) + g2[:, lanes].astype(f32)
        grad = total.astype(bf16)
        grad_ref[:, lanes] = grad
        scaled = grad.astype(f32) * pair_scale(since, pair, length)
        summary_ref[:, lanes] = dot(r, scaled.astype(bf16), (0, 0)).astype(bf16)


def gradients_kernel(
    x_ref, w_ref, r_ref, g_ref, rows_ref, columns_ref, entering_ref, leaving_ref,
    grad_input_ref, grad_write_ref, grad_read_ref,
):
    length = x_ref.shape[0]
    heads = rows_ref.shape[0]
    w = w_ref[...]
    r = r_ref[...]
    row = lax.broadcasted_iota(jnp.int32, (length, length), 0)
    column = lax.broadcasted_iota(jnp.int32, (length, length), 1)
    later = column >= row
    meets = jnp.where(later, dot(w, r, (1, 1)), 0.0)
    cumulative = columns_ref[...]
    since = jnp.exp(cumulative)
    to_end = jnp.exp(cumulative[length - 1 : length, :] - cumulative)
    half = low_half(length)
    weighted = jnp.zeros((length, length), f32)
    grad_write = jnp.zeros((length, STATE), f32)
    grad_read = jnp.zeros((length, STATE), f32)
    for pair in range(heads // 2):
        lanes = slice(pair * LANES, (pair + 1) * LANES)
        x = x_ref[:, lanes]
        g = g_ref[:, lanes]
        parts = []
        for head in (2 * pair, 2 * pair + 1):
            difference = rows_ref[head : head + 1, :] - cumulative[:, head : head + 1]
            within = jnp.exp(jnp.minimum(difference, 0.0))
            parts.append(dot((within * meets).astype(bf16), g, (1, 0)))
            mine = half if head % 2 == 0 else jnp.logical_not(half)
            own = jnp.where(mine, x, jnp.zeros_like(x))
            weighted = weighted + within * dot(own, g, (1, 1))
        end_scale = pair_scale(to_end, pair, length)
        leaving = leaving_ref[:, lanes]
        carried = dot(w, leaving, (1, 0)) * end_scale
        grad_input_ref[:, lanes] = (jnp.where(half, parts[0], parts[1]) + carried).astype(bf16)
        grad_write += dot((x.astype(f32) * end_scale).astype(bf16), leaving, (1, 1))
        scaled = (g.astype(f32) * pair_scale(since, pair, length)).astype(bf16)
        grad_read += dot(scaled, entering_ref[:, lanes], (1, 1))
    weighted = jnp.where(later, weighted, 0.0).astype(bf16)
    grad_write_ref[...] = (grad_write + dot(weighted, r, (1, 0))).astype(bf16)
    grad_read_ref[...] = (grad_read + dot(weighted, w, (0, 0))).astype(bf16)


def weight_kernel(
    c0, c1, c2, c3, m0, m1, m2, m3, mine_ref, other_ref, held, total, sems
):
    copies = []
    for m, ref in enumerate((c0, c1, c2, c3)):
        slot = lax.rem(lax.axis_index("tp") - lax.axis_index("dp") + 8 - m, 4)
        copy = pltpu.make_async_copy(ref, held.at[slot], sems.at[m])
        copy.start()
        copies.append(copy)
    for copy in copies:
        copy.wait()
    mixers = (m0, m3, m2, m1)
    acc = dot(held[0], mixers[0][...], (0, 0))
    for n in range(1, 4):
        acc = acc + dot(held[n], mixers[n][...], (0, 0))
    total[...] = acc
    ring, rows = mine_ref.shape[0], mine_ref.shape[1]
    core = lax.rem(lax.axis_index("ctx"), 2)
    for n in range(ring):
        start = pl.multiple_of((2 * n + core) * rows, rows)
        mine_ref[n] = total[pl.ds(start, rows), :].astype(bf16)
        start = pl.multiple_of((2 * n + 1 - core) * rows, rows)
        other_ref[n] = total[pl.ds(start, rows), :].astype(bf16)


def add_kernel(mine_ref, other_ref, out_ref):
    out_ref[...] = mine_ref[...].astype(f32) + other_ref[...].astype(f32)


def shape(dims, dtype=bf16):
    return jax.ShapeDtypeStruct(dims, dtype)


def per_device(
    head_input, write_vectors, read_vectors, log_decay, cotangent, out_weight, scale_exponent
):
    dp, ctx, tp = (lax.axis_size(name) for name in ("dp", "ctx", "tp"))
    x, w, r = head_input[0], write_vectors[0], read_vectors[0]
    length, columns = x.shape
    heads = log_decay.shape[1]

    def transposed(value):
        pairs = [(a * tp + k, k * tp + a) for a in range(dp) for k in range(tp)]
        return lax.ppermute(value, ("dp", "tp"), pairs)

    def along_tp(value, n):
        return lax.ppermute(value, "tp", [(i, (i + n) % tp) for i in range(tp)])

    def along_dp(value, n):
        return lax.ppermute(value, "dp", [(i, (i + n) % dp) for i in range(dp)])

    turned = transposed(cotangent[0])
    cots = [turned] + [along_tp(turned, m) for m in range(1, tp)]
    dequant = call(dequant_kernel, shape(out_weight.shape), 2)(out_weight, scale_exponent)
    weight = lax.all_gather(dequant, "ctx", axis=0, tiled=True)

    packed, cum_rows, cum_columns = call(
        state_kernel,
        [shape((STATE, columns + LANES)), shape((heads, length), f32), shape((length, LANES), f32)],
        3,
    )(x, w, log_decay[0])
    packed = lax.all_to_all(packed, "ctx", 0, 0, tiled=True)
    entering, decays = call(
        forward_scan_kernel, [shape((STATE, columns)), shape((ctx, columns), f32)], 1
    )(packed)
    entering = lax.all_to_all(entering, "ctx", 0, 0, tiled=True)

    mixer = call(mixer_kernel, shape((length, columns)), 6)(
        x, w, r, cum_rows, cum_columns, entering
    )
    mixer, weight = lax.optimization_barrier((mixer, weight))
    mixers = [mixer] + [along_dp(mixer, n) for n in range(1, dp)]

    vmem = pl.BlockSpec(memory_space=pltpu.VMEM)
    anywhere = pl.BlockSpec(memory_space=pl.ANY)
    model = cotangent.shape[2]
    parts = call(
        project_kernel,
        [shape((length, columns))] * 3 + [shape((length // 2, columns))] * 2,
        5,
        scratch=[pltpu.VMEM((dp, length, model), bf16), pltpu.SemaphoreType.DMA((dp,))],
        in_specs=[anywhere] * dp + [vmem],
    )(*cots, weight)
    top, bottom = along_dp(parts[3], 1), along_dp(parts[4], -1)
    folded = call(fold_kernel, [shape((length, columns))] * 2, 4, flops=40_000_000_000)(
        parts[1], parts[2], top, bottom
    )
    arrived = [along_dp(folded[0], 1), along_dp(folded[1], -1)]

    parts, mixers = lax.optimization_barrier((parts, mixers))
    rows = model // ctx
    mine, other = call(
        weight_kernel,
        [shape((ctx // 2, rows, columns))] * 2,
        8,
        flops=20_000_000_000,
        scratch=[
            pltpu.VMEM((dp, length, model), bf16),
            pltpu.VMEM((model, columns), f32),
            pltpu.SemaphoreType.DMA((dp,)),
        ],
        in_specs=[anywhere] * dp + [vmem] * dp,
    )(*cots, *mixers)
    other = lax.ppermute(other, "ctx", [(i, i ^ 1) for i in range(ctx)])
    total = call(add_kernel, shape((ctx // 2, rows, columns), f32), 2)(mine, other)
    chips = [[2 * k + core for k in range(ctx // 2)] for core in range(2)]
    grad_weight = lax.psum_scatter(total, "ctx", axis_index_groups=chips)
    grad, summary = call(
        adjoint_kernel,
        [shape((length, columns)), shape((STATE, columns))],
        5,
        flops=50_000_000_000,
    )(
        parts[0], *arrived, r, cum_columns
    )
    summary = lax.all_to_all(summary, "ctx", 0, 0, tiled=True)
    leaving = call(backward_scan_kernel, shape((STATE, columns)), 2)(summary, decays)
    leaving = lax.all_to_all(leaving, "ctx", 0, 0, tiled=True)
    grad_input, grad_write, grad_read = call(
        gradients_kernel,
        [shape((length, columns)), shape((length, STATE)), shape((length, STATE))],
        8,
    )(x, w, r, grad, cum_rows, cum_columns, entering, leaving)
    return grad_input[None], grad_write[None], grad_read[None], grad_weight


def solution(mesh):
    return jax.shard_map(
        per_device,
        mesh=mesh,
        in_specs=(
            P("dp", "ctx", "tp"),
            P("dp", "ctx", "tp"),
            P("dp", "ctx", "tp"),
            P("dp", "tp", "ctx"),
            P("dp", "ctx", "tp"),
            P(("dp", "ctx"), "tp"),
            P(("dp", "ctx"), "tp"),
        ),
        out_specs=(
            P("dp", "ctx", "tp"),
            P("dp", "ctx", "tp"),
            P("dp", "ctx", "tp"),
            P(("dp", "ctx"), "tp"),
        ),
        check_vma=False,
    )
```

```python
import functools

import jax
import jax.numpy as jnp
from jax import lax
from jax.experimental import pallas as pl
from jax.experimental.pallas import tpu as pltpu
from jax.sharding import PartitionSpec as P

HEADS = 64
GROUPS = 4
HEAD_DIM = 64
STATE = 128
SCALE_BLOCK = 32
LANES = 128
VMEM_LIMIT = 50 * 1024 * 1024

bf16 = jnp.bfloat16
f32 = jnp.float32
HIGHEST = lax.Precision.HIGHEST


def call(kernel, out_shape, n_in, flops=0, bytes_accessed=0, scratch=(), in_specs=None):
    out_specs = jax.tree.map(lambda _: pl.BlockSpec(memory_space=pltpu.VMEM), out_shape)
    return pl.pallas_call(
        kernel,
        out_shape=out_shape,
        in_specs=in_specs or [pl.BlockSpec(memory_space=pltpu.VMEM)] * n_in,
        out_specs=out_specs,
        scratch_shapes=list(scratch),
        compiler_params=pltpu.CompilerParams(vmem_limit_bytes=VMEM_LIMIT),
        cost_estimate=pl.CostEstimate(
            flops=flops, bytes_accessed=bytes_accessed, transcendentals=0
        ),
    )


def staged(kernel, out_shape, *args):
    def whole(value):
        return pl.BlockSpec(value.shape, lambda i: (0,) * len(value.shape))

    return pl.pallas_call(
        kernel,
        grid=(1,),
        out_shape=out_shape,
        in_specs=[whole(value) for value in args],
        out_specs=jax.tree.map(whole, out_shape),
        compiler_params=pltpu.CompilerParams(vmem_limit_bytes=VMEM_LIMIT),
    )(*args)


def dot(a, b, contract, precision=None):
    return lax.dot_general(
        a, b, ((contract[:1], contract[1:]), ((), ())),
        precision=precision, preferred_element_type=f32,
    )


def low_half(rows):
    return lax.broadcasted_iota(jnp.int32, (rows, LANES), 1) < HEAD_DIM


def pair_scale(columns, pair, rows):
    first = columns[:, 2 * pair : 2 * pair + 1]
    second = columns[:, 2 * pair + 1 : 2 * pair + 2]
    return jnp.where(low_half(rows), first, second)


def spread_matrix(heads):
    head = lax.broadcasted_iota(jnp.int32, (LANES, heads * HEAD_DIM), 0)
    column = lax.broadcasted_iota(jnp.int32, (LANES, heads * HEAD_DIM), 1)
    return jnp.where(column // HEAD_DIM == head, 1.0, 0.0).astype(f32)


def dequant_kernel(weight_ref, exponent_ref, out_ref):
    scales = jnp.exp2(exponent_ref[...].astype(f32))
    for block in range(scales.shape[0]):
        rows = slice(block * SCALE_BLOCK, (block + 1) * SCALE_BLOCK)
        out_ref[rows, :] = (
            weight_ref[rows, :].astype(f32) * scales[block : block + 1, :]
        ).astype(bf16)


def state_kernel(x_ref, w_ref, decay_ref, packed_ref, rows_ref, columns_ref):
    length, columns = x_ref.shape
    heads = decay_ref.shape[0]
    log_decay = decay_ref[...]
    row = lax.broadcasted_iota(jnp.int32, (length, length), 0)
    column = lax.broadcasted_iota(jnp.int32, (length, length), 1)
    upto = jnp.where(row <= column, 1.0, 0.0).astype(f32)
    cumulative = dot(log_decay, upto, (1, 0), HIGHEST)
    rows_ref[...] = cumulative
    padded = jnp.concatenate(
        [cumulative, jnp.zeros((LANES - heads, length), f32)], axis=0
    )
    turned = jnp.transpose(padded)
    columns_ref[...] = turned
    ends = turned[length - 1 : length, :]
    to_end = jnp.exp(ends - turned)
    w = w_ref[...]
    for pair in range(heads // 2):
        lanes = slice(pair * LANES, (pair + 1) * LANES)
        scaled = x_ref[:, lanes].astype(f32) * pair_scale(to_end, pair, length)
        packed_ref[:, lanes] = dot(w, scaled.astype(bf16), (0, 0)).astype(bf16)
    high = ends.astype(bf16).astype(f32)
    middle = (ends - high).astype(bf16).astype(f32)
    low = ends - high - middle
    which = lax.broadcasted_iota(jnp.int32, (STATE, LANES), 0) % 8
    terms = jnp.where(
        which == 0, high, jnp.where(which == 1, middle, jnp.where(which == 2, low, 0.0))
    )
    packed_ref[:, columns:] = terms.astype(bf16)


def forward_scan_kernel(packed_ref, entering_ref, decay_ref):
    rows, total = packed_ref.shape
    columns = entering_ref.shape[1]
    size = decay_ref.shape[0]
    chunk = rows // size
    everything = packed_ref[...].astype(f32)
    terms = everything[:, columns:]
    sums = [
        jnp.sum(terms[k * chunk : (k + 1) * chunk], axis=0, keepdims=True) for k in range(size)
    ]
    decays = jnp.exp(jnp.concatenate(sums, axis=0))
    spread = dot(decays, spread_matrix(columns // HEAD_DIM), (1, 0), HIGHEST)
    decay_ref[...] = spread
    carry = jnp.zeros((chunk, columns), f32)
    before = []
    for k in range(size):
        before.append(carry)
        carry = spread[k : k + 1] * carry + everything[k * chunk : (k + 1) * chunk, :columns]
    entering_ref[...] = jnp.concatenate(before, axis=0).astype(bf16)


def backward_scan_kernel(summary_ref, decay_ref, leaving_ref):
    rows, columns = summary_ref.shape
    size = decay_ref.shape[0]
    chunk = rows // size
    everything = summary_ref[...].astype(f32)
    spread = decay_ref[...]
    carry = jnp.zeros((chunk, columns), f32)
    after = [None] * size
    for k in range(size - 1, -1, -1):
        after[k] = carry
        carry = spread[k : k + 1] * carry + everything[k * chunk : (k + 1) * chunk]
    leaving_ref[...] = jnp.concatenate(after, axis=0).astype(bf16)


def mixer_kernel(x_ref, w_ref, r_ref, rows_ref, columns_ref, entering_ref, out_ref):
    length = x_ref.shape[0]
    heads = rows_ref.shape[0]
    r = r_ref[...]
    row = lax.broadcasted_iota(jnp.int32, (length, length), 0)
    column = lax.broadcasted_iota(jnp.int32, (length, length), 1)
    meets = jnp.where(row >= column, dot(r, w_ref[...], (1, 1)), 0.0)
    cumulative = columns_ref[...]
    since = jnp.exp(cumulative)
    half = low_half(length)
    for pair in range(heads // 2):
        lanes = slice(pair * LANES, (pair + 1) * LANES)
        x = x_ref[:, lanes]
        parts = []
        for head in (2 * pair, 2 * pair + 1):
            difference = cumulative[:, head : head + 1] - rows_ref[head : head + 1, :]
            mixing = jnp.exp(jnp.minimum(difference, 0.0)) * meets
            parts.append(dot(mixing.astype(bf16), x, (1, 0)))
        carried = dot(r, entering_ref[:, lanes], (1, 0)) * pair_scale(since, pair, length)
        out_ref[:, lanes] = (jnp.where(half, parts[0], parts[1]) + carried).astype(bf16)


def hold_slices(refs, held, sems):
    own, before, after, top, bottom = refs
    place = lax.axis_index("tp") - lax.axis_index("dp") + 8
    half = top.shape[0]
    copies = [
        pltpu.make_async_copy(own, held.at[lax.rem(place, 4)], sems.at[0]),
        pltpu.make_async_copy(before, held.at[lax.rem(place - 1, 4)], sems.at[1]),
        pltpu.make_async_copy(after, held.at[lax.rem(place + 1, 4)], sems.at[2]),
        pltpu.make_async_copy(top, held.at[lax.rem(place + 2, 4), pl.ds(0, half)], sems.at[3]),
        pltpu.make_async_copy(bottom, held.at[lax.rem(place + 2, 4), pl.ds(half, half)], sems.at[4]),
    ]
    for copy in copies:
        copy.start()
    for copy in copies:
        copy.wait()


def project_kernel(c0, c1, c2, c3, c4, weight_ref, o0, o1, o2, o3, o4, held, sems):
    hold_slices((c0, c1, c2, c3, c4), held, sems)
    weight = weight_ref[...]
    half = o3.shape[0]
    opposite = dot(held[2], weight, (1, 0)).astype(bf16)
    o3[...] = opposite[:half]
    o4[...] = opposite[half:]
    for n, out in ((1, o1), (3, o2), (0, o0)):
        out[...] = dot(held[n], weight, (1, 0)).astype(bf16)


def fold_kernel(p1, p2, top, bottom, o1, o2):
    half = top.shape[0]
    o1[:half, :] = (p1[:half, :].astype(f32) + top[...].astype(f32)).astype(bf16)
    o1[half:, :] = p1[half:, :]
    o2[:half, :] = p2[:half, :]
    o2[half:, :] = (p2[half:, :].astype(f32) + bottom[...].astype(f32)).astype(bf16)


def adjoint_kernel(g0, g1, g2, r_ref, columns_ref, grad_ref, summary_ref):
    length, columns = g0.shape
    heads = columns // HEAD_DIM
    since = jnp.exp(columns_ref[...])
    r = r_ref[...]
    for pair in range(heads // 2):
        lanes = slice(pair * LANES, (pair + 1) * LANES)
        total = g0[:, lanes].astype(f32) + g1[:, lanes].astype(f32) + g2[:, lanes].astype(f32)
        grad = total.astype(bf16)
        grad_ref[:, lanes] = grad
        scaled = grad.astype(f32) * pair_scale(since, pair, length)
        summary_ref[:, lanes] = dot(r, scaled.astype(bf16), (0, 0)).astype(bf16)


def local_kernel(
    x_ref, w_ref, r_ref, g_ref, rows_ref, columns_ref, entering_ref,
    input_ref, write_ref, grad_read_ref,
):
    length = x_ref.shape[0]
    heads = rows_ref.shape[0]
    w = w_ref[...]
    r = r_ref[...]
    row = lax.broadcasted_iota(jnp.int32, (length, length), 0)
    column = lax.broadcasted_iota(jnp.int32, (length, length), 1)
    later = column >= row
    meets = jnp.where(later, dot(w, r, (1, 1)), 0.0)
    cumulative = columns_ref[...]
    since = jnp.exp(cumulative)
    half = low_half(length)
    weighted = jnp.zeros((length, length), f32)
    grad_read = jnp.zeros((length, STATE), f32)
    for pair in range(heads // 2):
        lanes = slice(pair * LANES, (pair + 1) * LANES)
        x = x_ref[:, lanes]
        g = g_ref[:, lanes]
        parts = []
        for head in (2 * pair, 2 * pair + 1):
            difference = rows_ref[head : head + 1, :] - cumulative[:, head : head + 1]
            within = jnp.exp(jnp.minimum(difference, 0.0))
            parts.append(dot((within * meets).astype(bf16), g, (1, 0)))
            mine = half if head % 2 == 0 else jnp.logical_not(half)
            own = jnp.where(mine, x, jnp.zeros_like(x))
            weighted = weighted + within * dot(own, g, (1, 1))
        input_ref[:, lanes] = jnp.where(half, parts[0], parts[1])
        scaled = (g.astype(f32) * pair_scale(since, pair, length)).astype(bf16)
        grad_read += dot(scaled, entering_ref[:, lanes], (1, 1))
    weighted = jnp.where(later, weighted, 0.0).astype(bf16)
    write_ref[...] = dot(weighted, r, (1, 0))
    grad_read_ref[...] = (grad_read + dot(weighted, w, (0, 0))).astype(bf16)


def gradients_kernel(
    x_ref, w_ref, columns_ref, leaving_ref, input_ref, write_ref, grad_input_ref, grad_write_ref
):
    length, columns = x_ref.shape
    w = w_ref[...]
    cumulative = columns_ref[...]
    to_end = jnp.exp(cumulative[length - 1 : length, :] - cumulative)
    grad_write = write_ref[...]
    for pair in range(columns // LANES):
        lanes = slice(pair * LANES, (pair + 1) * LANES)
        scale = pair_scale(to_end, pair, length)
        leaving = leaving_ref[:, lanes]
        carried = dot(w, leaving, (1, 0)) * scale
        grad_input_ref[:, lanes] = (input_ref[:, lanes] + carried).astype(bf16)
        scaled = (x_ref[:, lanes].astype(f32) * scale).astype(bf16)
        grad_write += dot(scaled, leaving, (1, 1))
    grad_write_ref[...] = grad_write.astype(bf16)


def weight_kernel(
    c0, c1, c2, c3, c4, m0, m1, m2, m3, m4, mine_ref, other_ref, held, mixers, total, sems, mixer_sems
):
    half = m3.shape[0]
    places = (0, 3, 1, (2, pl.ds(0, half)), (2, pl.ds(half, half)))
    copies = [
        pltpu.make_async_copy(ref, mixers.at[place], mixer_sems.at[k])
        for k, (ref, place) in enumerate(zip((m0, m1, m2, m3, m4), places))
    ]
    for copy in copies:
        copy.start()
    hold_slices((c0, c1, c2, c3, c4), held, sems)
    for copy in copies:
        copy.wait()
    acc = dot(held[0], mixers[0], (0, 0))
    for n in range(1, 4):
        acc = acc + dot(held[n], mixers[n], (0, 0))
    total[...] = acc
    ring, rows = mine_ref.shape[0], mine_ref.shape[1]
    core = lax.rem(lax.axis_index("ctx"), 2)
    for n in range(ring):
        start = pl.multiple_of((2 * n + core) * rows, rows)
        mine_ref[n] = total[pl.ds(start, rows), :].astype(bf16)
        start = pl.multiple_of((2 * n + 1 - core) * rows, rows)
        other_ref[n] = total[pl.ds(start, rows), :].astype(bf16)


def add_kernel(mine_ref, other_ref, out_ref):
    out_ref[...] = mine_ref[...].astype(f32) + other_ref[...].astype(f32)


def ring_gather(value, along):
    half = value.shape[0] // 2
    before, after = along(value, 1), along(value, -1)
    return [value, before, after, along(before[:half], 1), along(after[half:], -1)]


def shape(dims, dtype=bf16):
    return jax.ShapeDtypeStruct(dims, dtype)


def per_device(
    head_input, write_vectors, read_vectors, log_decay, cotangent, out_weight, scale_exponent
):
    dp, ctx, tp = (lax.axis_size(name) for name in ("dp", "ctx", "tp"))
    x, w, r = head_input[0], write_vectors[0], read_vectors[0]
    length, columns = x.shape
    heads = log_decay.shape[1]

    def transposed(value):
        pairs = [(a * tp + k, k * tp + a) for a in range(dp) for k in range(tp)]
        return lax.ppermute(value, ("dp", "tp"), pairs)

    def along_tp(value, n):
        return lax.ppermute(value, "tp", [(i, (i + n) % tp) for i in range(tp)])

    def along_dp(value, n):
        return lax.ppermute(value, "dp", [(i, (i + n) % dp) for i in range(dp)])

    turned = transposed(cotangent[0])
    cots = ring_gather(turned, along_tp)
    dequant = staged(dequant_kernel, shape(out_weight.shape), out_weight, scale_exponent)
    weight = lax.all_gather(dequant, "ctx", axis=0, tiled=True)

    packed, cum_rows, cum_columns = staged(
        state_kernel,
        [shape((STATE, columns + LANES)), shape((heads, length), f32), shape((length, LANES), f32)],
        x, w, log_decay[0],
    )
    packed = lax.all_to_all(packed, "ctx", 0, 0, tiled=True)
    entering, decays = call(
        forward_scan_kernel, [shape((STATE, columns)), shape((ctx, columns), f32)], 1
    )(packed)
    entering = lax.all_to_all(entering, "ctx", 0, 0, tiled=True)

    mixer = call(mixer_kernel, shape((length, columns)), 6)(
        x, w, r, cum_rows, cum_columns, entering
    )
    mixer, weight = lax.optimization_barrier((mixer, weight))
    mixers = ring_gather(mixer, along_dp)

    vmem = pl.BlockSpec(memory_space=pltpu.VMEM)
    anywhere = pl.BlockSpec(memory_space=pl.ANY)
    model = cotangent.shape[2]
    parts = call(
        project_kernel,
        [shape((length, columns))] * 3 + [shape((length // 2, columns))] * 2,
        6,
        scratch=[pltpu.VMEM((dp, length, model), bf16), pltpu.SemaphoreType.DMA((5,))],
        in_specs=[anywhere] * 5 + [vmem],
    )(*cots, weight)
    top, bottom = along_dp(parts[3], 1), along_dp(parts[4], -1)
    folded = call(fold_kernel, [shape((length, columns))] * 2, 4, flops=40_000_000_000)(
        parts[1], parts[2], top, bottom
    )
    arrived = [along_dp(folded[0], 1), along_dp(folded[1], -1)]

    parts, mixers = lax.optimization_barrier((parts, mixers))
    rows = model // ctx
    mine, other = call(
        weight_kernel,
        [shape((ctx // 2, rows, columns))] * 2,
        8,
        flops=20_000_000_000,
        scratch=[
            pltpu.VMEM((dp, length, model), bf16),
            pltpu.VMEM((dp, length, columns), bf16),
            pltpu.VMEM((model, columns), f32),
            pltpu.SemaphoreType.DMA((5,)),
            pltpu.SemaphoreType.DMA((5,)),
        ],
        in_specs=[anywhere] * 10,
    )(*cots, *mixers)
    other = lax.ppermute(other, "ctx", [(i, i ^ 1) for i in range(ctx)])
    total = call(add_kernel, shape((ctx // 2, rows, columns), f32), 2)(mine, other)
    chips = [[2 * k + core for k in range(ctx // 2)] for core in range(2)]
    grad_weight = lax.psum_scatter(total, "ctx", axis_index_groups=chips)
    grad, summary = call(
        adjoint_kernel,
        [shape((length, columns)), shape((STATE, columns))],
        5,
        flops=50_000_000_000,
    )(
        parts[0], *arrived, r, cum_columns
    )
    summary = lax.all_to_all(summary, "ctx", 0, 0, tiled=True)
    leaving = call(backward_scan_kernel, shape((STATE, columns)), 2)(summary, decays)
    leaving = lax.all_to_all(leaving, "ctx", 0, 0, tiled=True)
    local_input, local_write, grad_read = call(
        local_kernel,
        [shape((length, columns), f32), shape((length, STATE), f32), shape((length, STATE))],
        7,
    )(x, w, r, grad, cum_rows, cum_columns, entering)
    grad_input, grad_write = call(
        gradients_kernel, [shape((length, columns)), shape((length, STATE))], 6
    )(x, w, cum_columns, leaving, local_input, local_write)
    return grad_input[None], grad_write[None], grad_read[None], grad_weight


def solution(mesh):
    return jax.shard_map(
        per_device,
        mesh=mesh,
        in_specs=(
            P("dp", "ctx", "tp"),
            P("dp", "ctx", "tp"),
            P("dp", "ctx", "tp"),
            P("dp", "tp", "ctx"),
            P("dp", "ctx", "tp"),
            P(("dp", "ctx"), "tp"),
            P(("dp", "ctx"), "tp"),
        ),
        out_specs=(
            P("dp", "ctx", "tp"),
            P("dp", "ctx", "tp"),
            P("dp", "ctx", "tp"),
            P(("dp", "ctx"), "tp"),
        ),
        check_vma=False,
    )
```

```python
import functools

import jax
import jax.numpy as jnp
from jax import lax
from jax.experimental import pallas as pl
from jax.experimental.pallas import tpu as pltpu
from jax.sharding import PartitionSpec as P

HEADS = 64
GROUPS = 4
HEAD_DIM = 64
STATE = 128
SCALE_BLOCK = 32
LANES = 128
VMEM_LIMIT = 50 * 1024 * 1024

bf16 = jnp.bfloat16
f32 = jnp.float32
HIGHEST = lax.Precision.HIGHEST


def call(kernel, out_shape, n_in, flops=0, bytes_accessed=0, scratch=(), in_specs=None, vmem=VMEM_LIMIT):
    out_specs = jax.tree.map(lambda _: pl.BlockSpec(memory_space=pltpu.VMEM), out_shape)
    return pl.pallas_call(
        kernel,
        out_shape=out_shape,
        in_specs=in_specs or [pl.BlockSpec(memory_space=pltpu.VMEM)] * n_in,
        out_specs=out_specs,
        scratch_shapes=list(scratch),
        compiler_params=pltpu.CompilerParams(vmem_limit_bytes=vmem),
        cost_estimate=pl.CostEstimate(
            flops=flops, bytes_accessed=bytes_accessed, transcendentals=0
        ),
    )


def fetched(kernel, out_shape, *args):
    count = len(args)

    def body(*refs):
        sources, results = refs[:count], refs[count : -count - 1]
        held, sems = refs[-count - 1 : -1], refs[-1]
        copies = [
            pltpu.make_async_copy(source, place, sems.at[k])
            for k, (source, place) in enumerate(zip(sources, held))
        ]
        for copy in copies:
            copy.start()
        for copy in copies:
            copy.wait()
        kernel(*held, *results)

    return call(
        body,
        out_shape,
        count,
        scratch=[pltpu.VMEM(value.shape, value.dtype) for value in args]
        + [pltpu.SemaphoreType.DMA((count,))],
        in_specs=[pl.BlockSpec(memory_space=pl.ANY)] * count,
        vmem=60 * 1024 * 1024,
    )(*args)


def dot(a, b, contract, precision=None):
    return lax.dot_general(
        a, b, ((contract[:1], contract[1:]), ((), ())),
        precision=precision, preferred_element_type=f32,
    )


def low_half(rows):
    return lax.broadcasted_iota(jnp.int32, (rows, LANES), 1) < HEAD_DIM


def pair_scale(columns, pair, rows):
    first = columns[:, 2 * pair : 2 * pair + 1]
    second = columns[:, 2 * pair + 1 : 2 * pair + 2]
    return jnp.where(low_half(rows), first, second)


def spread_matrix(heads):
    head = lax.broadcasted_iota(jnp.int32, (LANES, heads * HEAD_DIM), 0)
    column = lax.broadcasted_iota(jnp.int32, (LANES, heads * HEAD_DIM), 1)
    return jnp.where(column // HEAD_DIM == head, 1.0, 0.0).astype(f32)


def dequant_kernel(weight_ref, exponent_ref, out_ref):
    scales = jnp.exp2(exponent_ref[...].astype(f32))
    for block in range(scales.shape[0]):
        rows = slice(block * SCALE_BLOCK, (block + 1) * SCALE_BLOCK)
        out_ref[rows, :] = (
            weight_ref[rows, :].astype(f32) * scales[block : block + 1, :]
        ).astype(bf16)


def state_kernel(x_ref, w_ref, decay_ref, packed_ref, rows_ref, columns_ref):
    length, columns = x_ref.shape
    heads = decay_ref.shape[0]
    log_decay = decay_ref[...]
    row = lax.broadcasted_iota(jnp.int32, (length, length), 0)
    column = lax.broadcasted_iota(jnp.int32, (length, length), 1)
    upto = jnp.where(row <= column, 1.0, 0.0).astype(f32)
    cumulative = dot(log_decay, upto, (1, 0), HIGHEST)
    rows_ref[...] = cumulative
    padded = jnp.concatenate(
        [cumulative, jnp.zeros((LANES - heads, length), f32)], axis=0
    )
    turned = jnp.transpose(padded)
    columns_ref[...] = turned
    ends = turned[length - 1 : length, :]
    to_end = jnp.exp(ends - turned)
    w = w_ref[...]
    for pair in range(heads // 2):
        lanes = slice(pair * LANES, (pair + 1) * LANES)
        scaled = x_ref[:, lanes].astype(f32) * pair_scale(to_end, pair, length)
        packed_ref[:, lanes] = dot(w, scaled.astype(bf16), (0, 0)).astype(bf16)
    high = ends.astype(bf16).astype(f32)
    middle = (ends - high).astype(bf16).astype(f32)
    low = ends - high - middle
    which = lax.broadcasted_iota(jnp.int32, (STATE, LANES), 0) % 8
    terms = jnp.where(
        which == 0, high, jnp.where(which == 1, middle, jnp.where(which == 2, low, 0.0))
    )
    packed_ref[:, columns:] = terms.astype(bf16)


def forward_scan_kernel(packed_ref, entering_ref, decay_ref):
    rows, total = packed_ref.shape
    columns = entering_ref.shape[1]
    size = decay_ref.shape[0]
    chunk = rows // size
    everything = packed_ref[...].astype(f32)
    terms = everything[:, columns:]
    sums = [
        jnp.sum(terms[k * chunk : (k + 1) * chunk], axis=0, keepdims=True) for k in range(size)
    ]
    decays = jnp.exp(jnp.concatenate(sums, axis=0))
    spread = dot(decays, spread_matrix(columns // HEAD_DIM), (1, 0), HIGHEST)
    decay_ref[...] = spread
    carry = jnp.zeros((chunk, columns), f32)
    before = []
    for k in range(size):
        before.append(carry)
        carry = spread[k : k + 1] * carry + everything[k * chunk : (k + 1) * chunk, :columns]
    entering_ref[...] = jnp.concatenate(before, axis=0).astype(bf16)


def backward_scan_kernel(summary_ref, decay_ref, leaving_ref):
    rows, columns = summary_ref.shape
    size = decay_ref.shape[0]
    chunk = rows // size
    everything = summary_ref[...].astype(f32)
    spread = decay_ref[...]
    carry = jnp.zeros((chunk, columns), f32)
    after = [None] * size
    for k in range(size - 1, -1, -1):
        after[k] = carry
        carry = spread[k : k + 1] * carry + everything[k * chunk : (k + 1) * chunk]
    leaving_ref[...] = jnp.concatenate(after, axis=0).astype(bf16)


def mixer_kernel(x_ref, w_ref, r_ref, rows_ref, columns_ref, entering_ref, out_ref):
    length = x_ref.shape[0]
    heads = rows_ref.shape[0]
    r = r_ref[...]
    row = lax.broadcasted_iota(jnp.int32, (length, length), 0)
    column = lax.broadcasted_iota(jnp.int32, (length, length), 1)
    meets = jnp.where(row >= column, dot(r, w_ref[...], (1, 1)), 0.0)
    cumulative = columns_ref[...]
    since = jnp.exp(cumulative)
    half = low_half(length)
    for pair in range(heads // 2):
        lanes = slice(pair * LANES, (pair + 1) * LANES)
        x = x_ref[:, lanes]
        parts = []
        for head in (2 * pair, 2 * pair + 1):
            difference = cumulative[:, head : head + 1] - rows_ref[head : head + 1, :]
            mixing = jnp.exp(jnp.minimum(difference, 0.0)) * meets
            parts.append(dot(mixing.astype(bf16), x, (1, 0)))
        carried = dot(r, entering_ref[:, lanes], (1, 0)) * pair_scale(since, pair, length)
        out_ref[:, lanes] = (jnp.where(half, parts[0], parts[1]) + carried).astype(bf16)


def hold_slices(refs, held, sems):
    own, before, after, top, bottom = refs
    place = lax.axis_index("tp") - lax.axis_index("dp") + 8
    half = top.shape[0]
    copies = [
        pltpu.make_async_copy(own, held.at[lax.rem(place, 4)], sems.at[0]),
        pltpu.make_async_copy(before, held.at[lax.rem(place - 1, 4)], sems.at[1]),
        pltpu.make_async_copy(after, held.at[lax.rem(place + 1, 4)], sems.at[2]),
        pltpu.make_async_copy(top, held.at[lax.rem(place + 2, 4), pl.ds(0, half)], sems.at[3]),
        pltpu.make_async_copy(bottom, held.at[lax.rem(place + 2, 4), pl.ds(half, half)], sems.at[4]),
    ]
    for copy in copies:
        copy.start()
    for copy in copies:
        copy.wait()


def project_kernel(c0, c1, c2, c3, c4, weight_ref, o0, o1, o2, o3, o4, held, sems):
    hold_slices((c0, c1, c2, c3, c4), held, sems)
    weight = weight_ref[...]
    half = o3.shape[0]
    opposite = dot(held[2], weight, (1, 0)).astype(bf16)
    o3[...] = opposite[:half]
    o4[...] = opposite[half:]
    for n, out in ((1, o1), (3, o2), (0, o0)):
        out[...] = dot(held[n], weight, (1, 0)).astype(bf16)


def fold_kernel(p1, p2, top, bottom, o1, o2):
    half = top.shape[0]
    o1[:half, :] = (p1[:half, :].astype(f32) + top[...].astype(f32)).astype(bf16)
    o1[half:, :] = p1[half:, :]
    o2[:half, :] = p2[:half, :]
    o2[half:, :] = (p2[half:, :].astype(f32) + bottom[...].astype(f32)).astype(bf16)


def adjoint_kernel(g0, g1, g2, r_ref, columns_ref, grad_ref, summary_ref):
    length, columns = g0.shape
    heads = columns // HEAD_DIM
    since = jnp.exp(columns_ref[...])
    r = r_ref[...]
    for pair in range(heads // 2):
        lanes = slice(pair * LANES, (pair + 1) * LANES)
        total = g0[:, lanes].astype(f32) + g1[:, lanes].astype(f32) + g2[:, lanes].astype(f32)
        grad = total.astype(bf16)
        grad_ref[:, lanes] = grad
        scaled = grad.astype(f32) * pair_scale(since, pair, length)
        summary_ref[:, lanes] = dot(r, scaled.astype(bf16), (0, 0)).astype(bf16)


def local_kernel(
    x_ref, w_ref, r_ref, g_ref, rows_ref, columns_ref, entering_ref,
    input_ref, write_ref, grad_read_ref,
):
    length = x_ref.shape[0]
    heads = rows_ref.shape[0]
    w = w_ref[...]
    r = r_ref[...]
    row = lax.broadcasted_iota(jnp.int32, (length, length), 0)
    column = lax.broadcasted_iota(jnp.int32, (length, length), 1)
    later = column >= row
    meets = jnp.where(later, dot(w, r, (1, 1)), 0.0)
    cumulative = columns_ref[...]
    since = jnp.exp(cumulative)
    half = low_half(length)
    weighted = jnp.zeros((length, length), f32)
    grad_read = jnp.zeros((length, STATE), f32)
    for pair in range(heads // 2):
        lanes = slice(pair * LANES, (pair + 1) * LANES)
        x = x_ref[:, lanes]
        g = g_ref[:, lanes]
        parts = []
        for head in (2 * pair, 2 * pair + 1):
            difference = rows_ref[head : head + 1, :] - cumulative[:, head : head + 1]
            within = jnp.exp(jnp.minimum(difference, 0.0))
            parts.append(dot((within * meets).astype(bf16), g, (1, 0)))
            mine = half if head % 2 == 0 else jnp.logical_not(half)
            own = jnp.where(mine, x, jnp.zeros_like(x))
            weighted = weighted + within * dot(own, g, (1, 1))
        input_ref[:, lanes] = jnp.where(half, parts[0], parts[1])
        scaled = (g.astype(f32) * pair_scale(since, pair, length)).astype(bf16)
        grad_read += dot(scaled, entering_ref[:, lanes], (1, 1))
    weighted = jnp.where(later, weighted, 0.0).astype(bf16)
    write_ref[...] = dot(weighted, r, (1, 0))
    grad_read_ref[...] = (grad_read + dot(weighted, w, (0, 0))).astype(bf16)


def gradients_kernel(
    x_ref, w_ref, columns_ref, leaving_ref, input_ref, write_ref, grad_input_ref, grad_write_ref
):
    length, columns = x_ref.shape
    w = w_ref[...]
    cumulative = columns_ref[...]
    to_end = jnp.exp(cumulative[length - 1 : length, :] - cumulative)
    grad_write = write_ref[...]
    for pair in range(columns // LANES):
        lanes = slice(pair * LANES, (pair + 1) * LANES)
        scale = pair_scale(to_end, pair, length)
        leaving = leaving_ref[:, lanes]
        carried = dot(w, leaving, (1, 0)) * scale
        grad_input_ref[:, lanes] = (input_ref[:, lanes] + carried).astype(bf16)
        scaled = (x_ref[:, lanes].astype(f32) * scale).astype(bf16)
        grad_write += dot(scaled, leaving, (1, 1))
    grad_write_ref[...] = grad_write.astype(bf16)


def weight_kernel(
    c0, c1, c2, c3, c4, m0, m1, m2, m3, m4, mine_ref, other_ref, held, mixers, total, sems, mixer_sems
):
    half = m3.shape[0]
    places = (0, 3, 1, (2, pl.ds(0, half)), (2, pl.ds(half, half)))
    copies = [
        pltpu.make_async_copy(ref, mixers.at[place], mixer_sems.at[k])
        for k, (ref, place) in enumerate(zip((m0, m1, m2, m3, m4), places))
    ]
    for copy in copies:
        copy.start()
    hold_slices((c0, c1, c2, c3, c4), held, sems)
    for copy in copies:
        copy.wait()
    acc = dot(held[0], mixers[0], (0, 0))
    for n in range(1, 4):
        acc = acc + dot(held[n], mixers[n], (0, 0))
    total[...] = acc
    ring, rows = mine_ref.shape[0], mine_ref.shape[1]
    core = lax.rem(lax.axis_index("ctx"), 2)
    for n in range(ring):
        start = pl.multiple_of((2 * n + core) * rows, rows)
        mine_ref[n] = total[pl.ds(start, rows), :].astype(bf16)
        start = pl.multiple_of((2 * n + 1 - core) * rows, rows)
        other_ref[n] = total[pl.ds(start, rows), :].astype(bf16)


def add_kernel(mine_ref, other_ref, out_ref):
    out_ref[...] = mine_ref[...].astype(f32) + other_ref[...].astype(f32)


def ring_gather(value, along):
    half = value.shape[0] // 2
    before, after = along(value, 1), along(value, -1)
    return [value, before, after, along(before[:half], 1), along(after[half:], -1)]


def shape(dims, dtype=bf16):
    return jax.ShapeDtypeStruct(dims, dtype)


def per_device(
    head_input, write_vectors, read_vectors, log_decay, cotangent, out_weight, scale_exponent
):
    dp, ctx, tp = (lax.axis_size(name) for name in ("dp", "ctx", "tp"))
    x, w, r = head_input[0], write_vectors[0], read_vectors[0]
    length, columns = x.shape
    heads = log_decay.shape[1]

    def transposed(value):
        pairs = [(a * tp + k, k * tp + a) for a in range(dp) for k in range(tp)]
        return lax.ppermute(value, ("dp", "tp"), pairs)

    def along_tp(value, n):
        return lax.ppermute(value, "tp", [(i, (i + n) % tp) for i in range(tp)])

    def along_dp(value, n):
        return lax.ppermute(value, "dp", [(i, (i + n) % dp) for i in range(dp)])

    turned = transposed(cotangent[0])
    cots = ring_gather(turned, along_tp)
    dequant = fetched(dequant_kernel, shape(out_weight.shape), out_weight, scale_exponent)
    weight = lax.all_gather(dequant, "ctx", axis=0, tiled=True)

    packed, cum_rows, cum_columns = fetched(
        state_kernel,
        [shape((STATE, columns + LANES)), shape((heads, length), f32), shape((length, LANES), f32)],
        x, w, log_decay[0],
    )
    packed = lax.all_to_all(packed, "ctx", 0, 0, tiled=True)
    entering, decays = call(
        forward_scan_kernel, [shape((STATE, columns)), shape((ctx, columns), f32)], 1
    )(packed)
    entering = lax.all_to_all(entering, "ctx", 0, 0, tiled=True)

    mixer = call(mixer_kernel, shape((length, columns)), 6)(
        x, w, r, cum_rows, cum_columns, entering
    )
    mixer, weight = lax.optimization_barrier((mixer, weight))
    mixers = ring_gather(mixer, along_dp)

    vmem = pl.BlockSpec(memory_space=pltpu.VMEM)
    anywhere = pl.BlockSpec(memory_space=pl.ANY)
    model = cotangent.shape[2]
    parts = call(
        project_kernel,
        [shape((length, columns))] * 3 + [shape((length // 2, columns))] * 2,
        6,
        scratch=[pltpu.VMEM((dp, length, model), bf16), pltpu.SemaphoreType.DMA((5,))],
        in_specs=[anywhere] * 5 + [vmem],
    )(*cots, weight)
    top, bottom = along_dp(parts[3], 1), along_dp(parts[4], -1)
    folded = call(fold_kernel, [shape((length, columns))] * 2, 4, flops=40_000_000_000)(
        parts[1], parts[2], top, bottom
    )
    arrived = [along_dp(folded[0], 1), along_dp(folded[1], -1)]

    parts, mixers = lax.optimization_barrier((parts, mixers))
    rows = model // ctx
    mine, other = call(
        weight_kernel,
        [shape((ctx // 2, rows, columns))] * 2,
        8,
        flops=20_000_000_000,
        scratch=[
            pltpu.VMEM((dp, length, model), bf16),
            pltpu.VMEM((dp, length, columns), bf16),
            pltpu.VMEM((model, columns), f32),
            pltpu.SemaphoreType.DMA((5,)),
            pltpu.SemaphoreType.DMA((5,)),
        ],
        in_specs=[anywhere] * 10,
    )(*cots, *mixers)
    other = lax.ppermute(other, "ctx", [(i, i ^ 1) for i in range(ctx)])
    total = call(add_kernel, shape((ctx // 2, rows, columns), f32), 2)(mine, other)
    chips = [[2 * k + core for k in range(ctx // 2)] for core in range(2)]
    grad_weight = lax.psum_scatter(total, "ctx", axis_index_groups=chips)
    grad, summary = call(
        adjoint_kernel,
        [shape((length, columns)), shape((STATE, columns))],
        5,
        flops=50_000_000_000,
    )(
        parts[0], *arrived, r, cum_columns
    )
    summary = lax.all_to_all(summary, "ctx", 0, 0, tiled=True)
    leaving = call(backward_scan_kernel, shape((STATE, columns)), 2)(summary, decays)
    leaving = lax.all_to_all(leaving, "ctx", 0, 0, tiled=True)
    local_input, local_write, grad_read = call(
        local_kernel,
        [shape((length, columns), f32), shape((length, STATE), f32), shape((length, STATE))],
        7,
    )(x, w, r, grad, cum_rows, cum_columns, entering)
    grad_input, grad_write = call(
        gradients_kernel, [shape((length, columns)), shape((length, STATE))], 6
    )(x, w, cum_columns, leaving, local_input, local_write)
    return grad_input[None], grad_write[None], grad_read[None], grad_weight


def solution(mesh):
    return jax.shard_map(
        per_device,
        mesh=mesh,
        in_specs=(
            P("dp", "ctx", "tp"),
            P("dp", "ctx", "tp"),
            P("dp", "ctx", "tp"),
            P("dp", "tp", "ctx"),
            P("dp", "ctx", "tp"),
            P(("dp", "ctx"), "tp"),
            P(("dp", "ctx"), "tp"),
        ),
        out_specs=(
            P("dp", "ctx", "tp"),
            P("dp", "ctx", "tp"),
            P("dp", "ctx", "tp"),
            P(("dp", "ctx"), "tp"),
        ),
        check_vma=False,
    )
```

```python
import functools

import jax
import jax.numpy as jnp
from jax import lax
from jax.experimental import pallas as pl
from jax.experimental.pallas import tpu as pltpu
from jax.sharding import PartitionSpec as P

HEADS = 64
GROUPS = 4
HEAD_DIM = 64
STATE = 128
SCALE_BLOCK = 32
LANES = 128
VMEM_LIMIT = 50 * 1024 * 1024

bf16 = jnp.bfloat16
f32 = jnp.float32
HIGHEST = lax.Precision.HIGHEST


def call(kernel, out_shape, n_in, flops=0, bytes_accessed=0, scratch=(), in_specs=None, vmem=VMEM_LIMIT):
    out_specs = jax.tree.map(lambda _: pl.BlockSpec(memory_space=pltpu.VMEM), out_shape)
    return pl.pallas_call(
        kernel,
        out_shape=out_shape,
        in_specs=in_specs or [pl.BlockSpec(memory_space=pltpu.VMEM)] * n_in,
        out_specs=out_specs,
        scratch_shapes=list(scratch),
        compiler_params=pltpu.CompilerParams(vmem_limit_bytes=vmem),
        cost_estimate=pl.CostEstimate(
            flops=flops, bytes_accessed=bytes_accessed, transcendentals=0
        ),
    )


def fetched(kernel, out_shape, *args):
    count = len(args)

    def body(*refs):
        sources, results = refs[:count], refs[count : -count - 1]
        held, sems = refs[-count - 1 : -1], refs[-1]
        copies = [
            pltpu.make_async_copy(source, place, sems.at[k])
            for k, (source, place) in enumerate(zip(sources, held))
        ]
        for copy in copies:
            copy.start()
        for copy in copies:
            copy.wait()
        kernel(*held, *results)

    return call(
        body,
        out_shape,
        count,
        scratch=[pltpu.VMEM(value.shape, value.dtype) for value in args]
        + [pltpu.SemaphoreType.DMA((count,))],
        in_specs=[pl.BlockSpec(memory_space=pl.ANY)] * count,
        vmem=60 * 1024 * 1024,
    )(*args)


def dot(a, b, contract, precision=None):
    return lax.dot_general(
        a, b, ((contract[:1], contract[1:]), ((), ())),
        precision=precision, preferred_element_type=f32,
    )


def low_half(rows):
    return lax.broadcasted_iota(jnp.int32, (rows, LANES), 1) < HEAD_DIM


def pair_scale(columns, pair, rows):
    first = columns[:, 2 * pair : 2 * pair + 1]
    second = columns[:, 2 * pair + 1 : 2 * pair + 2]
    return jnp.where(low_half(rows), first, second)


def spread_matrix(heads):
    head = lax.broadcasted_iota(jnp.int32, (LANES, heads * HEAD_DIM), 0)
    column = lax.broadcasted_iota(jnp.int32, (LANES, heads * HEAD_DIM), 1)
    return jnp.where(column // HEAD_DIM == head, 1.0, 0.0).astype(f32)


def dequant_kernel(weight_ref, exponent_ref, out_ref):
    scales = jnp.exp2(exponent_ref[...].astype(f32))
    for block in range(scales.shape[0]):
        rows = slice(block * SCALE_BLOCK, (block + 1) * SCALE_BLOCK)
        out_ref[rows, :] = (
            weight_ref[rows, :].astype(f32) * scales[block : block + 1, :]
        ).astype(bf16)


def state_kernel(x_ref, w_ref, decay_ref, packed_ref, rows_ref, columns_ref):
    length, columns = x_ref.shape
    heads = decay_ref.shape[0]
    log_decay = decay_ref[...]
    row = lax.broadcasted_iota(jnp.int32, (length, length), 0)
    column = lax.broadcasted_iota(jnp.int32, (length, length), 1)
    upto = jnp.where(row <= column, 1.0, 0.0).astype(f32)
    cumulative = dot(log_decay, upto, (1, 0), HIGHEST)
    rows_ref[...] = cumulative
    padded = jnp.concatenate(
        [cumulative, jnp.zeros((LANES - heads, length), f32)], axis=0
    )
    turned = jnp.transpose(padded)
    columns_ref[...] = turned
    ends = turned[length - 1 : length, :]
    to_end = jnp.exp(ends - turned)
    w = w_ref[...]
    for pair in range(heads // 2):
        lanes = slice(pair * LANES, (pair + 1) * LANES)
        scaled = x_ref[:, lanes].astype(f32) * pair_scale(to_end, pair, length)
        packed_ref[:, lanes] = dot(w, scaled.astype(bf16), (0, 0)).astype(bf16)
    high = ends.astype(bf16).astype(f32)
    middle = (ends - high).astype(bf16).astype(f32)
    low = ends - high - middle
    which = lax.broadcasted_iota(jnp.int32, (STATE, LANES), 0) % 8
    terms = jnp.where(
        which == 0, high, jnp.where(which == 1, middle, jnp.where(which == 2, low, 0.0))
    )
    packed_ref[:, columns:] = terms.astype(bf16)


def forward_scan_kernel(packed_ref, entering_ref, decay_ref):
    rows, total = packed_ref.shape
    columns = entering_ref.shape[1]
    size = decay_ref.shape[0]
    chunk = rows // size
    everything = packed_ref[...].astype(f32)
    terms = everything[:, columns:]
    sums = [
        jnp.sum(terms[k * chunk : (k + 1) * chunk], axis=0, keepdims=True) for k in range(size)
    ]
    decays = jnp.exp(jnp.concatenate(sums, axis=0))
    spread = dot(decays, spread_matrix(columns // HEAD_DIM), (1, 0), HIGHEST)
    decay_ref[...] = spread
    carry = jnp.zeros((chunk, columns), f32)
    before = []
    for k in range(size):
        before.append(carry)
        carry = spread[k : k + 1] * carry + everything[k * chunk : (k + 1) * chunk, :columns]
    entering_ref[...] = jnp.concatenate(before, axis=0).astype(bf16)


def backward_scan_kernel(summary_ref, decay_ref, leaving_ref):
    rows, columns = summary_ref.shape
    size = decay_ref.shape[0]
    chunk = rows // size
    everything = summary_ref[...].astype(f32)
    spread = decay_ref[...]
    carry = jnp.zeros((chunk, columns), f32)
    after = [None] * size
    for k in range(size - 1, -1, -1):
        after[k] = carry
        carry = spread[k : k + 1] * carry + everything[k * chunk : (k + 1) * chunk]
    leaving_ref[...] = jnp.concatenate(after, axis=0).astype(bf16)


def mixer_kernel(x_ref, w_ref, r_ref, rows_ref, columns_ref, entering_ref, out_ref):
    length = x_ref.shape[0]
    heads = rows_ref.shape[0]
    r = r_ref[...]
    row = lax.broadcasted_iota(jnp.int32, (length, length), 0)
    column = lax.broadcasted_iota(jnp.int32, (length, length), 1)
    meets = jnp.where(row >= column, dot(r, w_ref[...], (1, 1)), 0.0)
    cumulative = columns_ref[...]
    since = jnp.exp(cumulative)
    half = low_half(length)
    for pair in range(heads // 2):
        lanes = slice(pair * LANES, (pair + 1) * LANES)
        x = x_ref[:, lanes]
        parts = []
        for head in (2 * pair, 2 * pair + 1):
            difference = cumulative[:, head : head + 1] - rows_ref[head : head + 1, :]
            mixing = jnp.exp(jnp.minimum(difference, 0.0)) * meets
            parts.append(dot(mixing.astype(bf16), x, (1, 0)))
        carried = dot(r, entering_ref[:, lanes], (1, 0)) * pair_scale(since, pair, length)
        out_ref[:, lanes] = (jnp.where(half, parts[0], parts[1]) + carried).astype(bf16)


def hold_slices(refs, held, sems):
    own, before, after, top, bottom = refs
    place = lax.axis_index("tp") - lax.axis_index("dp") + 8
    half = top.shape[0]
    copies = [
        pltpu.make_async_copy(own, held.at[lax.rem(place, 4)], sems.at[0]),
        pltpu.make_async_copy(before, held.at[lax.rem(place - 1, 4)], sems.at[1]),
        pltpu.make_async_copy(after, held.at[lax.rem(place + 1, 4)], sems.at[2]),
        pltpu.make_async_copy(top, held.at[lax.rem(place + 2, 4), pl.ds(0, half)], sems.at[3]),
        pltpu.make_async_copy(bottom, held.at[lax.rem(place + 2, 4), pl.ds(half, half)], sems.at[4]),
    ]
    for copy in copies:
        copy.start()
    for copy in copies:
        copy.wait()


def project_kernel(c0, c1, c2, c3, c4, weight_ref, o0, o1, o2, o3, o4, held, sems):
    hold_slices((c0, c1, c2, c3, c4), held, sems)
    weight = weight_ref[...]
    half = o3.shape[0]
    opposite = dot(held[2], weight, (1, 0)).astype(bf16)
    o3[...] = opposite[:half]
    o4[...] = opposite[half:]
    for n, out in ((1, o1), (3, o2), (0, o0)):
        out[...] = dot(held[n], weight, (1, 0)).astype(bf16)


def fold_kernel(p1, p2, top, bottom, o1, o2):
    half = top.shape[0]
    o1[:half, :] = (p1[:half, :].astype(f32) + top[...].astype(f32)).astype(bf16)
    o1[half:, :] = p1[half:, :]
    o2[:half, :] = p2[:half, :]
    o2[half:, :] = (p2[half:, :].astype(f32) + bottom[...].astype(f32)).astype(bf16)


def adjoint_kernel(g0, g1, g2, r_ref, columns_ref, grad_ref, summary_ref):
    length, columns = g0.shape
    heads = columns // HEAD_DIM
    since = jnp.exp(columns_ref[...])
    r = r_ref[...]
    for pair in range(heads // 2):
        lanes = slice(pair * LANES, (pair + 1) * LANES)
        total = g0[:, lanes].astype(f32) + g1[:, lanes].astype(f32) + g2[:, lanes].astype(f32)
        grad = total.astype(bf16)
        grad_ref[:, lanes] = grad
        scaled = grad.astype(f32) * pair_scale(since, pair, length)
        summary_ref[:, lanes] = dot(r, scaled.astype(bf16), (0, 0)).astype(bf16)


def local_kernel(
    x_ref, w_ref, r_ref, g_ref, rows_ref, columns_ref, entering_ref,
    input_ref, write_ref, grad_read_ref,
):
    length = x_ref.shape[0]
    heads = rows_ref.shape[0]
    w = w_ref[...]
    r = r_ref[...]
    row = lax.broadcasted_iota(jnp.int32, (length, length), 0)
    column = lax.broadcasted_iota(jnp.int32, (length, length), 1)
    later = column >= row
    meets = jnp.where(later, dot(w, r, (1, 1)), 0.0)
    cumulative = columns_ref[...]
    since = jnp.exp(cumulative)
    half = low_half(length)
    weighted = jnp.zeros((length, length), f32)
    grad_read = jnp.zeros((length, STATE), f32)
    for pair in range(heads // 2):
        lanes = slice(pair * LANES, (pair + 1) * LANES)
        x = x_ref[:, lanes]
        g = g_ref[:, lanes]
        parts = []
        for head in (2 * pair, 2 * pair + 1):
            difference = rows_ref[head : head + 1, :] - cumulative[:, head : head + 1]
            within = jnp.exp(jnp.minimum(difference, 0.0))
            parts.append(dot((within * meets).astype(bf16), g, (1, 0)))
            mine = half if head % 2 == 0 else jnp.logical_not(half)
            own = jnp.where(mine, x, jnp.zeros_like(x))
            weighted = weighted + within * dot(own, g, (1, 1))
        input_ref[:, lanes] = jnp.where(half, parts[0], parts[1])
        scaled = (g.astype(f32) * pair_scale(since, pair, length)).astype(bf16)
        grad_read += dot(scaled, entering_ref[:, lanes], (1, 1))
    weighted = jnp.where(later, weighted, 0.0).astype(bf16)
    write_ref[...] = dot(weighted, r, (1, 0))
    grad_read_ref[...] = (grad_read + dot(weighted, w, (0, 0))).astype(bf16)


def gradients_kernel(
    x_ref, w_ref, columns_ref, leaving_ref, input_ref, write_ref, grad_input_ref, grad_write_ref
):
    length, columns = x_ref.shape
    w = w_ref[...]
    cumulative = columns_ref[...]
    to_end = jnp.exp(cumulative[length - 1 : length, :] - cumulative)
    grad_write = write_ref[...]
    for pair in range(columns // LANES):
        lanes = slice(pair * LANES, (pair + 1) * LANES)
        scale = pair_scale(to_end, pair, length)
        leaving = leaving_ref[:, lanes]
        carried = dot(w, leaving, (1, 0)) * scale
        grad_input_ref[:, lanes] = (input_ref[:, lanes] + carried).astype(bf16)
        scaled = (x_ref[:, lanes].astype(f32) * scale).astype(bf16)
        grad_write += dot(scaled, leaving, (1, 1))
    grad_write_ref[...] = grad_write.astype(bf16)


def weight_kernel(
    c0, c1, c2, c3, c4, m0, m1, m2, m3, m4, mine_ref, other_ref, held, mixers, total, sems, mixer_sems
):
    half = m3.shape[0]
    places = (0, 3, 1, (2, pl.ds(0, half)), (2, pl.ds(half, half)))
    copies = [
        pltpu.make_async_copy(ref, mixers.at[place], mixer_sems.at[k])
        for k, (ref, place) in enumerate(zip((m0, m1, m2, m3, m4), places))
    ]
    for copy in copies:
        copy.start()
    hold_slices((c0, c1, c2, c3, c4), held, sems)
    for copy in copies:
        copy.wait()
    acc = dot(held[0], mixers[0], (0, 0))
    for n in range(1, 4):
        acc = acc + dot(held[n], mixers[n], (0, 0))
    total[...] = acc
    ring, rows = mine_ref.shape[0], mine_ref.shape[1]
    core = lax.rem(lax.axis_index("ctx"), 2)
    for n in range(ring):
        start = pl.multiple_of((2 * n + core) * rows, rows)
        mine_ref[n] = total[pl.ds(start, rows), :].astype(bf16)
        start = pl.multiple_of((2 * n + 1 - core) * rows, rows)
        other_ref[n] = total[pl.ds(start, rows), :].astype(bf16)


def add_kernel(mine_ref, other_ref, out_ref):
    out_ref[...] = mine_ref[...].astype(f32) + other_ref[...].astype(f32)


def ring_gather(value, along):
    half = value.shape[0] // 2
    before, after = along(value, 1), along(value, -1)
    return [value, before, after, along(before[:half], 1), along(after[half:], -1)]


def shape(dims, dtype=bf16):
    return jax.ShapeDtypeStruct(dims, dtype)


def per_device(
    head_input, write_vectors, read_vectors, log_decay, cotangent, out_weight, scale_exponent
):
    dp, ctx, tp = (lax.axis_size(name) for name in ("dp", "ctx", "tp"))
    x, w, r = head_input[0], write_vectors[0], read_vectors[0]
    length, columns = x.shape
    heads = log_decay.shape[1]

    def transposed(value):
        pairs = [(a * tp + k, k * tp + a) for a in range(dp) for k in range(tp)]
        return lax.ppermute(value, ("dp", "tp"), pairs)

    def along_tp(value, n):
        return lax.ppermute(value, "tp", [(i, (i + n) % tp) for i in range(tp)])

    def along_dp(value, n):
        return lax.ppermute(value, "dp", [(i, (i + n) % dp) for i in range(dp)])

    turned = transposed(cotangent[0])
    cots = ring_gather(turned, along_tp)
    dequant = fetched(dequant_kernel, shape(out_weight.shape), out_weight, scale_exponent)
    weight = lax.all_gather(dequant, "ctx", axis=0, tiled=True)

    packed, cum_rows, cum_columns = fetched(
        state_kernel,
        [shape((STATE, columns + LANES)), shape((heads, length), f32), shape((length, LANES), f32)],
        x, w, log_decay[0],
    )
    packed = lax.all_to_all(packed, "ctx", 0, 0, tiled=True)
    entering, decays = call(
        forward_scan_kernel,
        [shape((STATE, columns)), shape((ctx, columns), f32)],
        1,
        flops=5_000_000_000,
    )(packed)
    entering = lax.all_to_all(entering, "ctx", 0, 0, tiled=True)

    mixer = call(mixer_kernel, shape((length, columns)), 6)(
        x, w, r, cum_rows, cum_columns, entering
    )
    mixer, weight = lax.optimization_barrier((mixer, weight))
    mixers = ring_gather(mixer, along_dp)

    vmem = pl.BlockSpec(memory_space=pltpu.VMEM)
    anywhere = pl.BlockSpec(memory_space=pl.ANY)
    model = cotangent.shape[2]
    parts = call(
        project_kernel,
        [shape((length, columns))] * 3 + [shape((length // 2, columns))] * 2,
        6,
        scratch=[pltpu.VMEM((dp, length, model), bf16), pltpu.SemaphoreType.DMA((5,))],
        in_specs=[anywhere] * 5 + [vmem],
    )(*cots, weight)
    top, bottom = along_dp(parts[3], 1), along_dp(parts[4], -1)
    folded = call(fold_kernel, [shape((length, columns))] * 2, 4, flops=40_000_000_000)(
        parts[1], parts[2], top, bottom
    )
    arrived = [along_dp(folded[0], 1), along_dp(folded[1], -1)]

    parts, mixers = lax.optimization_barrier((parts, mixers))
    rows = model // ctx
    mine, other = call(
        weight_kernel,
        [shape((ctx // 2, rows, columns))] * 2,
        8,
        flops=20_000_000_000,
        scratch=[
            pltpu.VMEM((dp, length, model), bf16),
            pltpu.VMEM((dp, length, columns), bf16),
            pltpu.VMEM((model, columns), f32),
            pltpu.SemaphoreType.DMA((5,)),
            pltpu.SemaphoreType.DMA((5,)),
        ],
        in_specs=[anywhere] * 10,
    )(*cots, *mixers)
    other = lax.ppermute(other, "ctx", [(i, i ^ 1) for i in range(ctx)])
    total = call(add_kernel, shape((ctx // 2, rows, columns), f32), 2)(mine, other)
    chips = [[2 * k + core for k in range(ctx // 2)] for core in range(2)]
    grad_weight = lax.psum_scatter(total, "ctx", axis_index_groups=chips)
    grad, summary = call(
        adjoint_kernel,
        [shape((length, columns)), shape((STATE, columns))],
        5,
        flops=50_000_000_000,
    )(
        parts[0], *arrived, r, cum_columns
    )
    summary = lax.all_to_all(summary, "ctx", 0, 0, tiled=True)
    leaving = call(backward_scan_kernel, shape((STATE, columns)), 2)(summary, decays)
    leaving = lax.all_to_all(leaving, "ctx", 0, 0, tiled=True)
    local_input, local_write, grad_read = call(
        local_kernel,
        [shape((length, columns), f32), shape((length, STATE), f32), shape((length, STATE))],
        7,
    )(x, w, r, grad, cum_rows, cum_columns, entering)
    grad_input, grad_write = call(
        gradients_kernel, [shape((length, columns)), shape((length, STATE))], 6
    )(x, w, cum_columns, leaving, local_input, local_write)
    return grad_input[None], grad_write[None], grad_read[None], grad_weight


def solution(mesh):
    return jax.shard_map(
        per_device,
        mesh=mesh,
        in_specs=(
            P("dp", "ctx", "tp"),
            P("dp", "ctx", "tp"),
            P("dp", "ctx", "tp"),
            P("dp", "tp", "ctx"),
            P("dp", "ctx", "tp"),
            P(("dp", "ctx"), "tp"),
            P(("dp", "ctx"), "tp"),
        ),
        out_specs=(
            P("dp", "ctx", "tp"),
            P("dp", "ctx", "tp"),
            P("dp", "ctx", "tp"),
            P(("dp", "ctx"), "tp"),
        ),
        check_vma=False,
    )
```
